128 devices in a mesh: tm: 4 (over y), clus: 32 (over z, x, core).
Axes of the slice: x: 4, y: 4, z: 4, core: 2. Of those that a mesh axis runs over, the one named last changes fastest.
Arguments:
- embedding: bfloat16 [131072, 384], P(('tm', 'clus')), may hold values from -6 to 6
- cluster_of: int32 [131072], P(('tm', 'clus')), may hold values from 0 to 255, as said below
Outputs:
- mixed: bfloat16 [131072, 384], P(('tm', 'clus'))
The draws below stay inside these ranges and needn't reach their ends.
Inputs may be any that keep to these rules, and one draw needn't show every extreme that they name: `cluster_of`: of the 1024 invoices of one device at most 16 belong to the two clusters of one owner, and on every device some owner receives exactly 16; each cluster holds at most 1024 invoices, and in every draw both clusters of some owner hold exactly 1024.
All inputs are finite; a program needn't handle non-finite values.
Results may differ from the reference program's by a relative error of at most 0.0035.
Values may be sent and summed in bfloat16 or wider, within the bound.
A program may use at most 64 MiB of HBM per device.

```python
import jax
import jax.numpy as jnp
from jax import lax

E = 384
ROWS_DEV = 1024
OWNERS = 128
NCL = 256
SLOT = 16
CAP = 1024
TOKENS = 131072


def draw_cluster_of(key, part):
    key = jax.random.fold_in(key, 11)
    half = OWNERS // 2
    share = SLOT // 2
    key_pair, key_pick, key_sign, key_full, key_split, key_order = jax.random.split(key, 6)
    offset = jax.random.randint(key_pair, (OWNERS, half), -share, share + 1)
    picked = jax.random.randint(key_pick, (OWNERS,), 0, half)
    signs = jax.random.randint(key_sign, (OWNERS,), 0, 2) * 2 - 1
    columns = jnp.arange(half)[None, :]
    offset = jnp.where(columns == picked[:, None], signs[:, None] * share, offset)
    fullest = jax.random.randint(key_full, (), 0, OWNERS)
    full_sign = jnp.where(fullest < half, 1, -1)
    offset = jnp.where(columns == fullest % half, full_sign * share, offset)
    counts = jnp.concatenate([share + offset, share - offset], axis=1)
    lowest = jnp.maximum(counts - share, 0)
    highest = jnp.minimum(counts, share)
    spread = jax.random.randint(key_split, (OWNERS, OWNERS), 0, 1 << 20)
    first = lowest + spread % (highest - lowest + 1)
    ends = jnp.cumsum(counts, axis=1)
    starts = ends - counts
    places = jnp.arange(ROWS_DEV)
    owner = jax.vmap(lambda edge: jnp.searchsorted(edge, places, side='right'))(ends)
    within = places[None, :] - jnp.take_along_axis(starts, owner, axis=1)
    second = (within >= jnp.take_along_axis(first, owner, axis=1)).astype(jnp.int32)
    cluster = (owner * 2 + second).astype(jnp.int32)
    shuffles = jax.vmap(lambda sub: jax.random.permutation(sub, ROWS_DEV))(jax.random.split(key_order, OWNERS))
    cluster = jnp.take_along_axis(cluster, shuffles, axis=1)
    return cluster.reshape(TOKENS).astype(jnp.int32)


def steps_of(key, shape, pieces, least, high):
    def one(dim, blocks):
        draws = jax.random.uniform(jax.random.fold_in(jax.random.fold_in(key, 6), dim), (blocks,), jnp.float32, least / len(pieces), high / len(pieces))
        return jnp.repeat(jnp.exp(draws), shape[dim] // blocks).reshape((-1,) + (1,) * (len(shape) - dim - 1))

    factor_of = one(*pieces[0])
    for cut in pieces[1:]:
        factor_of = factor_of * one(*cut)
    return factor_of


def scatter_about(key, shape, deviation, reach, shards=(), kind=jnp.bfloat16):
    level = steps_of(key, shape, shards, -0.22, 0.18) if shards else 1.0
    drawn = jax.random.normal(key, shape, jnp.float32) * deviation * level
    return jnp.minimum(jnp.maximum(drawn, -reach), reach).astype(kind)


def setup_inputs(seed: int = 0) -> dict:
    keys = jax.random.split(jax.random.key(seed), 3)
    return {
        "embedding": scatter_about(keys[0], (TOKENS, E), 1.0, 6.0, ((0, 128),)),
        "cluster_of": draw_cluster_of(jax.random.fold_in(keys[2], 71), 0),
    }


TAU = 40.0

def unit_rows(rows):
    values = rows.astype(jnp.float32)
    return (values * lax.rsqrt(lax.optimization_barrier(jnp.sum(values * values, axis=1, keepdims=True)) + 1e-06)).astype(jnp.bfloat16)

def cluster_result(rows, units, present, count, use_skip):
    capacity, width = rows.shape
    block = capacity // 4
    totals = [jnp.zeros((block, width), jnp.float32) for index in range(4)]
    masses = [jnp.zeros((block,), jnp.float32) for index in range(4)]
    inner = jnp.arange(block, dtype=jnp.int32)
    for left in range(4):
        for right in range(left, 4):
            units_left = units[left * block:(left + 1) * block]
            units_right = units[right * block:(right + 1) * block]
            rows_left = rows[left * block:(left + 1) * block]
            rows_right = rows[right * block:(right + 1) * block]
            keep = present[left * block:(left + 1) * block][:, None] & present[right * block:(right + 1) * block][None, :]
            if left == right:
                keep = keep & (inner[:, None] != inner[None, :])

            def scored(unused, units_left=units_left, units_right=units_right, rows_left=rows_left, rows_right=rows_right, keep=keep, diagonal=left == right):
                scores = jnp.dot(units_left, units_right.T, preferred_element_type=jnp.float32)
                weight = jnp.where(keep, jnp.exp(TAU * scores), jnp.zeros((), jnp.float32)).astype(jnp.bfloat16)
                wide = weight.astype(jnp.float32)
                total_left = jnp.dot(weight, rows_right, preferred_element_type=jnp.float32)
                mass_left = lax.optimization_barrier(jnp.sum(wide, axis=1))
                if diagonal:
                    return (total_left, mass_left, jnp.zeros_like(total_left), jnp.zeros_like(mass_left))
                total_right = lax.dot_general(weight, rows_left, (((0,), (0,)), ((), ())), preferred_element_type=jnp.float32)
                return (total_left, mass_left, total_right, lax.optimization_barrier(jnp.sum(wide, axis=0)))

            def skipped(unused):
                empty = jnp.zeros((block, width), jnp.float32)
                none = jnp.zeros((block,), jnp.float32)
                return (empty, none, empty, none)
            if use_skip:
                parts = lax.cond(count > right * block, scored, skipped, None)
            else:
                parts = scored(None)
            totals[left] = totals[left] + parts[0]
            masses[left] = masses[left] + parts[1]
            if left != right:
                totals[right] = totals[right] + parts[2]
                masses[right] = masses[right] + parts[3]
    total = jnp.concatenate(totals, axis=0)
    mass = jnp.concatenate(masses, axis=0)
    return (rows.astype(jnp.float32) - total / (1.0 + mass)[:, None]).astype(jnp.bfloat16)

def reference(embedding, cluster_of):
    total_rows = embedding.shape[0]
    order = jnp.argsort(cluster_of, stable=True).astype(jnp.int32)
    counts = jax.ops.segment_sum(jnp.ones((total_rows,), jnp.int32), cluster_of, num_segments=NCL).astype(jnp.int32)
    starts = (jnp.cumsum(counts) - counts).astype(jnp.int32)
    units = unit_rows(embedding)
    sorted_rows = embedding[order]
    sorted_units = units[order]
    slots = jnp.arange(CAP, dtype=jnp.int32)

    def visit(cluster, result):
        index = starts[cluster] + slots
        present = slots < counts[cluster]
        safe = jnp.minimum(index, total_rows - 1).astype(jnp.int32)
        rows = jnp.where(present[:, None], sorted_rows[safe], jnp.zeros((), embedding.dtype))
        units_here = jnp.where(present[:, None], sorted_units[safe], jnp.zeros((), units.dtype))
        mixed = cluster_result(rows, units_here, present, counts[cluster], True)
        target = jnp.where(present, order[safe], total_rows).astype(jnp.int32)
        return result.at[target].set(mixed.astype(result.dtype), mode='drop')
    return lax.fori_loop(0, NCL, visit, jnp.zeros_like(embedding))
```

```python
import functools
import math

import jax
import jax.numpy as jnp
from jax import lax
from jax.experimental import pallas as pl
from jax.experimental.pallas import tpu as pltpu
from jax.sharding import PartitionSpec as P

MESH = pl.DeviceIdType.MESH
BF16, F32, I32 = jnp.bfloat16, jnp.float32, jnp.int32
N = 128
ROWS = 1024
E = 384
SLOT = 16
SLOTS = N * SLOT
CH = 256
NCH = SLOTS // CH
PER = CH // SLOT
STEP, BACK = 37, 45
SCALE = 40.0 * math.log2(math.e)
APART = 16.0


def rank_of(shift):
    return (shift * BACK) & (N - 1)


def coords():
    tm, cl = lax.axis_index("tm"), lax.axis_index("clus")
    return tm, cl // 8, (cl // 2) % 4, cl % 2


def partner(k, sign):
    shift = (k * STEP) % N
    y, z, x, c = coords()
    y = (y + 4 + sign * (shift // 32)) % 4
    z = (z + 4 + sign * ((shift // 8) % 4)) % 4
    x = (x + 4 + sign * ((shift // 2) % 4)) % 4
    c = (c + shift) % 2
    return (y, z * 8 + x * 2 + c)


def at(start, size):
    return pl.ds(pl.multiple_of(start, 16), size)


def kernel(
    emb, labels, out,
    send, meta_send, recv, meta_recv, rows, left, right, total, result, returned, pick,
    send_sem, meta_send_sem, back_sem, recv_sem, meta_sem, return_sem,
):
    barrier = pltpu.get_barrier_semaphore()

    def greet(k, carry):
        pl.semaphore_signal(barrier, inc=1, device_id=partner(k, 1), device_id_type=MESH)
        return carry

    lax.fori_loop(1, N, greet, 0)

    y, z, x, c = coords()
    label = labels[...]
    owner = label >> 1
    dy, dz = ((owner >> 5) - y) & 3, ((owner >> 3) - z) & 3
    dx, dc = ((owner >> 1) - x) & 3, (owner - c) & 1
    order = rank_of(dy * 32 + dz * 8 + dx * 2 + dc)
    hits = (order == lax.broadcasted_iota(I32, (N, ROWS), 0)).astype(F32)
    upper = (
        lax.broadcasted_iota(I32, (CH, CH), 0) <= lax.broadcasted_iota(I32, (CH, CH), 1)
    ).astype(BF16)
    before = jnp.zeros((N, 1), F32)
    ranks = []
    for part in range(ROWS // CH):
        hit = hits[:, part * CH : (part + 1) * CH]
        count = jnp.dot(hit.astype(BF16), upper, preferred_element_type=F32) + before
        ranks.append(jnp.sum(count * hit, axis=0, keepdims=True))
        before = before + jnp.sum(hit, axis=1, keepdims=True)
    rank = jnp.concatenate(ranks, axis=1).astype(I32) - 1
    target = order * SLOT + rank

    lane_of = lax.broadcasted_iota(I32, (N, ROWS), 0)
    value = jnp.where(lane_of == rank, (label & 1) + 1, 0).astype(BF16)
    meta = lax.dot_general(
        hits.astype(BF16), value, (((1,), (1,)), ((), ())), preferred_element_type=F32
    )
    meta_send[...] = meta.astype(I32).reshape(N, 1, N)

    pl.semaphore_wait(barrier, N - 1)

    def send_one(k, carry):
        device = partner(k, 1)
        chunk = k // PER
        pltpu.make_async_remote_copy(
            src_ref=meta_send.at[k], dst_ref=meta_recv.at[k],
            send_sem=meta_send_sem, recv_sem=meta_sem.at[chunk],
            device_id=device, device_id_type=MESH,
        ).start()
        pltpu.make_async_remote_copy(
            src_ref=send.at[at(k * SLOT, SLOT)], dst_ref=recv.at[at(k * SLOT, SLOT)],
            send_sem=send_sem, recv_sem=recv_sem.at[chunk],
            device_id=device, device_id_type=MESH,
        ).start()
        return carry

    def pack(chunk, carry):
        slot = lax.broadcasted_iota(I32, (CH, ROWS), 0) + chunk * CH
        chosen = (slot == target).astype(BF16)
        packed = jnp.dot(chosen, emb[...], preferred_element_type=F32)
        send[at(chunk * CH, CH), :] = packed.astype(BF16)
        lax.fori_loop(jnp.maximum(chunk * PER, 1), (chunk + 1) * PER, send_one, 0)
        return carry

    lax.fori_loop(0, NCH, pack, 0)

    column = jnp.broadcast_to(target, (N, ROWS)).T
    lanes = lax.broadcasted_iota(I32, (ROWS, N), 1)
    for part in range(SLOTS // N):
        pick[:, part * N : (part + 1) * N] = (column == lanes + part * N).astype(BF16)

    rows[:, E:] = jnp.ones((SLOTS, N), BF16)
    diagonal = lax.broadcasted_iota(I32, (CH, CH), 0) == lax.broadcasted_iota(I32, (CH, CH), 1)
    lane = lax.broadcasted_iota(I32, (CH, N), 1)
    own_slot = lax.broadcasted_iota(I32, (PER, SLOT, N), 1) == lax.broadcasted_iota(
        I32, (PER, SLOT, N), 2
    )
    spread = jnp.ones((N, N), BF16)

    def weights(a, b):
        score = lax.dot_general(
            left[at(a * CH, CH), :], right[at(b * CH, CH), :],
            (((1,), (1,)), ((), ())), preferred_element_type=F32,
        )
        return jnp.exp2(score * SCALE)

    for chunk in range(NCH):
        first = 1 if chunk == 0 else 0
        base, count = chunk * CH + first * SLOT, CH - first * SLOT
        here = slice(chunk * CH, (chunk + 1) * CH)
        pltpu.make_async_copy(
            meta_recv.at[chunk * PER + first : (chunk + 1) * PER],
            meta_recv.at[chunk * PER + first : (chunk + 1) * PER],
            meta_sem.at[chunk],
        ).wait()
        pltpu.make_async_copy(
            recv.at[base : base + count], recv.at[base : base + count], recv_sem.at[chunk]
        ).wait()
        if chunk == 0:
            recv[0:SLOT, :] = send[0:SLOT, :]
            meta_recv[0] = meta_send[0]
        marks = meta_recv[chunk * PER : (chunk + 1) * PER].reshape(PER, 1, N)
        marks = jnp.where(own_slot, jnp.broadcast_to(marks, (PER, SLOT, N)), 0)
        marks = marks.astype(F32).reshape(CH, N).astype(BF16)
        kind = jnp.dot(marks, spread, preferred_element_type=F32).astype(I32)
        kind = jnp.where(kind == 0, 2, kind - 1)
        values = recv[here, :]
        wide = values.astype(F32)
        unit = wide * lax.rsqrt(jnp.sum(wide * wide, axis=1, keepdims=True) + 1e-06)
        unit = unit.astype(BF16)
        rows[here, :E] = values
        left[here, :E] = unit
        right[here, :E] = unit
        left[here, E:] = ((lane < 3) & (lane != kind)).astype(BF16)
        right[here, E:] = jnp.where(lane == kind, -APART, 0.0).astype(BF16)

        own = jnp.where(diagonal, 0.0, weights(chunk, chunk)).astype(BF16)
        total[here, :] = jnp.dot(own, rows[here, :], preferred_element_type=F32)

        def earlier(b, carry, chunk=chunk, here=here):
            there = at(b * CH, CH)
            weight = weights(chunk, b).astype(BF16)
            total[here, :] += jnp.dot(weight, rows[there, :], preferred_element_type=F32)
            return carry

        lax.fori_loop(0, chunk, earlier, 0)

        def later(b, carry, chunk=chunk, here=here):
            there = at(b * CH, CH)
            weight = weights(b, chunk).astype(BF16)
            total[there, :] += jnp.dot(weight, rows[here, :], preferred_element_type=F32)
            return carry

        if chunk < NCH - 1:
            lax.fori_loop(0, chunk, later, 0)

    def return_one(k, carry):
        pltpu.make_async_remote_copy(
            src_ref=result.at[at(k * SLOT, SLOT)], dst_ref=returned.at[at(k * SLOT, SLOT)],
            send_sem=back_sem, recv_sem=return_sem.at[k // PER],
            device_id=partner(k, -1), device_id_type=MESH,
        ).start()
        return carry

    def finish(b, carry):
        there = at(b * CH, CH)
        full = total[there, :]

        def last(full):
            weight = weights(b, NCH - 1).astype(BF16)
            return full + jnp.dot(
                weight, rows[(NCH - 1) * CH :, :], preferred_element_type=F32
            )

        full = lax.cond(b < NCH - 1, last, lambda full: full, full)
        inverse = 1.0 / (1.0 + full[:, E:])
        for part in range(E // N):
            span = slice(part * N, (part + 1) * N)
            mixed = recv[there, span].astype(F32) - full[:, span] * inverse
            result[there, span] = mixed.astype(BF16)
        lax.fori_loop(jnp.maximum(b * PER, 1), (b + 1) * PER, return_one, 0)
        return carry

    lax.fori_loop(0, NCH, finish, 0)
    returned[0:SLOT, :] = result[0:SLOT, :]

    for chunk in range(NCH):
        first = 1 if chunk == 0 else 0
        base, count = chunk * CH + first * SLOT, CH - first * SLOT
        here = slice(chunk * CH, (chunk + 1) * CH)
        pltpu.make_async_copy(
            returned.at[base : base + count], returned.at[base : base + count],
            return_sem.at[chunk],
        ).wait()
        part = jnp.dot(pick[:, here], returned[here, :], preferred_element_type=F32).astype(BF16)
        if chunk == 0:
            out[...] = part
        else:
            out[...] += part

    sent = slice(SLOT, SLOTS)
    pltpu.make_async_copy(send.at[sent], send.at[sent], send_sem).wait()
    pltpu.make_async_copy(meta_send.at[1:N], meta_send.at[1:N], meta_send_sem).wait()
    pltpu.make_async_copy(result.at[sent], result.at[sent], back_sem).wait()


def on_device(embedding, cluster_of):
    return pl.pallas_call(
        kernel,
        out_shape=jax.ShapeDtypeStruct((ROWS, E), BF16),
        in_specs=[pl.BlockSpec(memory_space=pltpu.VMEM)] * 2,
        out_specs=pl.BlockSpec(memory_space=pltpu.VMEM),
        scratch_shapes=[
            pltpu.VMEM((SLOTS, E), BF16),
            pltpu.VMEM((N, 1, N), I32),
            pltpu.VMEM((SLOTS, E), BF16),
            pltpu.VMEM((N, 1, N), I32),
            pltpu.VMEM((SLOTS, E + N), BF16),
            pltpu.VMEM((SLOTS, E + N), BF16),
            pltpu.VMEM((SLOTS, E + N), BF16),
            pltpu.VMEM((SLOTS, E + N), F32),
            pltpu.VMEM((SLOTS, E), BF16),
            pltpu.VMEM((SLOTS, E), BF16),
            pltpu.VMEM((ROWS, SLOTS), BF16),
            pltpu.SemaphoreType.DMA,
            pltpu.SemaphoreType.DMA,
            pltpu.SemaphoreType.DMA,
            pltpu.SemaphoreType.DMA((NCH,)),
            pltpu.SemaphoreType.DMA((NCH,)),
            pltpu.SemaphoreType.DMA((NCH,)),
        ],
        compiler_params=pltpu.CompilerParams(
            collective_id=0, has_side_effects=True, vmem_limit_bytes=56 << 20
        ),
    )(embedding, cluster_of.reshape(1, ROWS))


def solution(mesh):
    return jax.shard_map(
        on_device,
        mesh=mesh,
        in_specs=(P(("tm", "clus"), None), P(("tm", "clus"))),
        out_specs=P(("tm", "clus"), None),
        check_vma=False,
    )
```

```python
import jax
import jax.numpy as jnp
from jax import lax
from jax.experimental import pallas as pl
from jax.experimental.pallas import tpu as pltpu
from jax.sharding import PartitionSpec as P

MESH = pl.DeviceIdType.MESH
BF16, F32, I32 = jnp.bfloat16, jnp.float32, jnp.int32
N = 128
ROWS = 1024
E = 384
SLOT = 16
SLOTS = N * SLOT
CH = 256
NCH = SLOTS // CH
PER = CH // SLOT
STEP, BACK = 91, 83
APART = 16.0


def rank_of(shift):
    return (shift * BACK) & (N - 1)


def coords():
    tm, cl = lax.axis_index("tm"), lax.axis_index("clus")
    return tm, cl // 8, (cl // 2) % 4, cl % 2


def partner(k, sign):
    shift = lax.rem(k * STEP, N)
    dy, dz, dx = lax.div(shift, 32), lax.rem(lax.div(shift, 8), 4), lax.rem(lax.div(shift, 2), 4)
    y, z, x, c = coords()
    if sign < 0:
        dy, dz, dx = 4 - dy, 4 - dz, 4 - dx
    y, z, x, c = lax.rem(y + dy, 4), lax.rem(z + dz, 4), lax.rem(x + dx, 4), lax.rem(c + shift, 2)
    return (y, z * 8 + x * 2 + c)


def at(start, size):
    return pl.ds(pl.multiple_of(start, 16), size)


def kernel(
    emb_hbm, labels, out,
    emb, send, meta_send, recv, meta_recv, rows, left, right, total, result, returned, pick,
    fetch_sem, planes_sem, send_sem, meta_send_sem, back_sem, recv_sem, meta_sem, return_sem,
):
    fetch = pltpu.make_async_copy(emb_hbm, emb, fetch_sem)
    fetch.start()

    y, z, x, c = coords()
    barrier = pltpu.get_barrier_semaphore()
    plane = [(a, b) for a in range(4) for b in range(4) if (a, b) != (0, 0)]
    line = [(a, b) for a in range(4) for b in range(2) if (a, b) != (0, 0)]
    ys, zs = [lax.rem(y + d, 4) for d in range(4)], [lax.rem(z + d, 4) * 8 for d in range(4)]
    xs, cs = [lax.rem(x + d, 4) * 2 for d in range(4)], [c, 1 - c]
    for a, b in plane:
        pl.semaphore_signal(
            barrier, inc=1, device_id=(ys[a], zs[b] + (xs[0] + c)), device_id_type=MESH
        )
    for a, b in line:
        pl.semaphore_signal(
            barrier, inc=1, device_id=(y, zs[0] + (xs[a] + cs[b])), device_id_type=MESH
        )

    label = labels[...]
    owner = label >> 1
    dy, dz = ((owner >> 5) - y) & 3, ((owner >> 3) - z) & 3
    dx, dc = ((owner >> 1) - x) & 3, (owner - c) & 1
    order = rank_of(dy * 32 + dz * 8 + dx * 2 + dc)
    hits = (order == lax.broadcasted_iota(I32, (N, ROWS), 0)).astype(F32)
    upper = (
        lax.broadcasted_iota(I32, (CH, CH), 0) <= lax.broadcasted_iota(I32, (CH, CH), 1)
    ).astype(BF16)
    before = jnp.zeros((N, 1), F32)
    ranks = []
    for part in range(ROWS // CH):
        hit = hits[:, part * CH : (part + 1) * CH]
        count = jnp.dot(hit.astype(BF16), upper, preferred_element_type=F32) + before
        ranks.append(jnp.sum(count * hit, axis=0, keepdims=True))
        before = before + jnp.sum(hit, axis=1, keepdims=True)
    rank = jnp.concatenate(ranks, axis=1).astype(I32) - 1
    target = order * SLOT + rank

    lane_of = lax.broadcasted_iota(I32, (N, ROWS), 0)
    value = jnp.where(lane_of == rank, (label & 1) + 1, 0).astype(BF16)
    meta = lax.dot_general(
        hits.astype(BF16), value, (((1,), (1,)), ((), ())), preferred_element_type=F32
    )
    meta_send[...] = meta.astype(I32).reshape(N, 1, N)

    def pack(chunk):
        slot = lax.broadcasted_iota(I32, (CH, ROWS), 0) + chunk * CH
        chosen = (slot == target).astype(BF16)
        packed = jnp.dot(chosen, emb[...], preferred_element_type=F32)
        send[chunk * CH : (chunk + 1) * CH, :] = packed.astype(BF16)

    fetch.wait()
    pack(0)
    pl.semaphore_wait(barrier, len(plane) + len(line))
    for a, b in line:
        pl.semaphore_signal(
            planes_sem, inc=1, device_id=(y, zs[0] + (xs[a] + cs[b])), device_id_type=MESH
        )
    pack(1)
    pl.semaphore_wait(planes_sem, len(line))

    def send_one(k, carry):
        device = partner(k, 1)
        chunk = k // PER
        pltpu.make_async_remote_copy(
            src_ref=meta_send.at[k], dst_ref=meta_recv.at[k],
            send_sem=meta_send_sem, recv_sem=meta_sem.at[chunk],
            device_id=device, device_id_type=MESH,
        ).start()
        pltpu.make_async_remote_copy(
            src_ref=send.at[at(k * SLOT, SLOT)], dst_ref=recv.at[at(k * SLOT, SLOT)],
            send_sem=send_sem, recv_sem=recv_sem.at[chunk],
            device_id=device, device_id_type=MESH,
        ).start()
        return carry

    for chunk in range(NCH):
        lax.fori_loop(max(chunk * PER, 1), (chunk + 1) * PER, send_one, 0)
        if 1 <= chunk < NCH - 1:
            pack(chunk + 1)

    column = jnp.broadcast_to(target, (N, ROWS)).T
    lanes = lax.broadcasted_iota(I32, (ROWS, N), 1)
    for part in range(SLOTS // N):
        pick[:, part * N : (part + 1) * N] = (column == lanes + part * N).astype(BF16)

    rows[:, E:] = jnp.ones((SLOTS, N), BF16)
    diagonal = lax.broadcasted_iota(I32, (CH, CH), 0) == lax.broadcasted_iota(I32, (CH, CH), 1)
    lane = lax.broadcasted_iota(I32, (CH, N), 1)
    own_slot = lax.broadcasted_iota(I32, (PER, SLOT, N), 1) == lax.broadcasted_iota(
        I32, (PER, SLOT, N), 2
    )
    spread = jnp.ones((N, N), BF16)

    def block(start, size, cols):
        parts = []
        for col in cols:
            score = lax.dot_general(
                left[start : start + size, :], right[col * CH : (col + 1) * CH, :],
                (((1,), (1,)), ((), ())), preferred_element_type=F32,
            )
            weight = jnp.exp(score * 40.0)
            if start == col * CH:
                weight = jnp.where(diagonal, 0.0, weight)
            parts.append(weight.astype(BF16))
        weight = parts[0] if len(parts) == 1 else jnp.concatenate(parts, axis=1)
        return jnp.dot(
            weight, rows[cols[0] * CH : (cols[-1] + 1) * CH, :], preferred_element_type=F32
        )

    def arrive(chunk):
        first = 1 if chunk == 0 else 0
        base, count = chunk * CH + first * SLOT, CH - first * SLOT
        here = slice(chunk * CH, (chunk + 1) * CH)
        pltpu.make_async_copy(
            meta_recv.at[chunk * PER + first : (chunk + 1) * PER],
            meta_recv.at[chunk * PER + first : (chunk + 1) * PER],
            meta_sem.at[chunk],
        ).wait()
        pltpu.make_async_copy(
            recv.at[base : base + count], recv.at[base : base + count], recv_sem.at[chunk]
        ).wait()
        if chunk == 0:
            recv[0:SLOT, :] = send[0:SLOT, :]
            meta_recv[0] = meta_send[0]
        marks = meta_recv[chunk * PER : (chunk + 1) * PER].reshape(PER, 1, N)
        marks = jnp.where(own_slot, jnp.broadcast_to(marks, (PER, SLOT, N)), 0)
        marks = marks.astype(F32).reshape(CH, N).astype(BF16)
        kind = jnp.dot(marks, spread, preferred_element_type=F32).astype(I32)
        kind = jnp.where(kind == 0, 2, kind - 1)
        values = recv[here, :]
        wide = values.astype(F32)
        unit = wide * lax.rsqrt(jnp.sum(wide * wide, axis=1, keepdims=True) + 1e-06)
        unit = unit.astype(BF16)
        rows[here, :E] = values
        left[here, :E] = unit
        right[here, :E] = unit
        left[here, E:] = ((lane < 3) & (lane != kind)).astype(BF16)
        right[here, E:] = jnp.where(lane == kind, -APART, 0.0).astype(BF16)

    for chunk in range(NCH - 1):
        arrive(chunk)
        here = slice(chunk * CH, (chunk + 1) * CH)
        total[here, :] = block(chunk * CH, CH, range(chunk + 1))
        for start in range(0, chunk * CH, 2 * CH):
            size = min(2 * CH, chunk * CH - start)
            total[start : start + size, :] += block(start, size, range(chunk, chunk + 1))
    arrive(NCH - 1)

    def return_one(k, carry):
        pltpu.make_async_remote_copy(
            src_ref=result.at[at(k * SLOT, SLOT)], dst_ref=returned.at[at(k * SLOT, SLOT)],
            send_sem=back_sem, recv_sem=return_sem.at[k // PER],
            device_id=partner(k, -1), device_id_type=MESH,
        ).start()
        return carry

    for chunk in range(NCH):
        here = slice(chunk * CH, (chunk + 1) * CH)
        if chunk < NCH - 1:
            full = total[here, :] + block(chunk * CH, CH, range(NCH - 1, NCH))
        else:
            full = block(chunk * CH, CH, range(NCH))
        inverse = 1.0 / (1.0 + full[:, E:])
        for part in range(E // N):
            span = slice(part * N, (part + 1) * N)
            mixed = rows[here, span].astype(F32) - full[:, span] * inverse
            result[here, span] = mixed.astype(BF16)
        lax.fori_loop(max(chunk * PER, 1), (chunk + 1) * PER, return_one, 0)
    returned[0:SLOT, :] = result[0:SLOT, :]

    for chunk in range(NCH):
        first = 1 if chunk == 0 else 0
        base, count = chunk * CH + first * SLOT, CH - first * SLOT
        here = slice(chunk * CH, (chunk + 1) * CH)
        pltpu.make_async_copy(
            returned.at[base : base + count], returned.at[base : base + count],
            return_sem.at[chunk],
        ).wait()
        part = jnp.dot(pick[:, here], returned[here, :], preferred_element_type=F32).astype(BF16)
        if chunk == 0:
            out[...] = part
        else:
            out[...] += part

    sent = slice(SLOT, SLOTS)
    pltpu.make_async_copy(send.at[sent], send.at[sent], send_sem).wait()
    pltpu.make_async_copy(meta_send.at[1:N], meta_send.at[1:N], meta_send_sem).wait()
    pltpu.make_async_copy(result.at[sent], result.at[sent], back_sem).wait()


def on_device(embedding, cluster_of):
    return pl.pallas_call(
        kernel,
        out_shape=jax.ShapeDtypeStruct((ROWS, E), BF16),
        in_specs=[
            pl.BlockSpec(memory_space=pl.ANY),
            pl.BlockSpec(memory_space=pltpu.VMEM),
        ],
        out_specs=pl.BlockSpec(memory_space=pltpu.VMEM),
        scratch_shapes=[
            pltpu.VMEM((ROWS, E), BF16),
            pltpu.VMEM((SLOTS, E), BF16),
            pltpu.VMEM((N, 1, N), I32),
            pltpu.VMEM((SLOTS, E), BF16),
            pltpu.VMEM((N, 1, N), I32),
            pltpu.VMEM((SLOTS, E + N), BF16),
            pltpu.VMEM((SLOTS, E + N), BF16),
            pltpu.VMEM((SLOTS, E + N), BF16),
            pltpu.VMEM((SLOTS, E + N), F32),
            pltpu.VMEM((SLOTS, E), BF16),
            pltpu.VMEM((SLOTS, E), BF16),
            pltpu.VMEM((ROWS, SLOTS), BF16),
            pltpu.SemaphoreType.DMA,
            pltpu.SemaphoreType.REGULAR,
            pltpu.SemaphoreType.DMA,
            pltpu.SemaphoreType.DMA,
            pltpu.SemaphoreType.DMA,
            pltpu.SemaphoreType.DMA((NCH,)),
            pltpu.SemaphoreType.DMA((NCH,)),
            pltpu.SemaphoreType.DMA((NCH,)),
        ],
        compiler_params=pltpu.CompilerParams(
            collective_id=0, has_side_effects=True, vmem_limit_bytes=56 << 20
        ),
    )(embedding, cluster_of.reshape(1, ROWS))


def solution(mesh):
    return jax.shard_map(
        on_device,
        mesh=mesh,
        in_specs=(P(("tm", "clus"), None), P(("tm", "clus"))),
        out_specs=P(("tm", "clus"), None),
        check_vma=False,
    )
```

```python
import jax
import jax.numpy as jnp
from jax import lax
from jax.experimental import pallas as pl
from jax.experimental.pallas import tpu as pltpu
from jax.sharding import PartitionSpec as P

MESH = pl.DeviceIdType.MESH
BF16, F32, I32 = jnp.bfloat16, jnp.float32, jnp.int32
N = 128
ROWS = 1024
E = 384
SLOT = 16
SLOTS = N * SLOT
CH = 256
NCH = SLOTS // CH
PER = CH // SLOT
NEAR = 23
EARLY = 4
APART = 16.0


def shift_of(k):
    if k < NEAR:
        turn, mate = (0, k // 3) if k % 3 == 0 else (k - k // 3, 0)
    else:
        turn, mate = (k - 16) // 7, (k - 16) % 7 + 1
    place = turn * 7 % 16
    return place // 4, place % 4, mate // 2, mate % 2


def order_of(dy, dz, dx, dc):
    turn, mate = ((dy * 4 + dz) * 7) & 15, dx * 2 + dc
    near = jnp.where(mate == 0, turn + (jnp.maximum(turn - 1, 0) >> 1), 3 * mate)
    return jnp.where((mate == 0) | (turn == 0), near, 15 + 7 * turn + mate)


def kernel(
    emb_hbm, labels_hbm, out,
    emb, labels, send, meta_send, recv, meta_recv, rows, left, right, total, result, returned, pick,
    fetch_sem, labels_sem, planes_sem,
    send_sem, meta_send_sem, back_sem, recv_sem, meta_sem, return_sem,
):
    fetch_labels = pltpu.make_async_copy(labels_hbm, labels, labels_sem)
    fetch_labels.start()
    fetch = pltpu.make_async_copy(emb_hbm, emb, fetch_sem)
    fetch.start()

    tm, cl = lax.axis_index("tm"), lax.axis_index("clus")
    y, z, x, c = tm, cl // 8, (cl // 2) % 4, cl % 2
    ys, zs = [lax.rem(y + d, 4) for d in range(4)], [lax.rem(z + d, 4) * 8 for d in range(4)]
    xs, cs = [lax.rem(x + d, 4) * 2 for d in range(4)], [c, 1 - c]
    barrier = pltpu.get_barrier_semaphore()

    def partner(k, sign):
        dy, dz, dx, dc = shift_of(k)
        return (ys[sign * dy % 4], zs[sign * dz % 4] + (xs[sign * dx % 4] + cs[dc]))

    def tell(sem, k):
        pl.semaphore_signal(sem, inc=1, device_id=partner(k, 1), device_id_type=MESH)

    for k in range(1, NEAR):
        tell(barrier, k)

    fetch_labels.wait()
    label = labels[...]
    owner = label >> 1
    dy, dz = ((owner >> 5) - y) & 3, ((owner >> 3) - z) & 3
    dx, dc = ((owner >> 1) - x) & 3, (owner - c) & 1
    order = order_of(dy, dz, dx, dc)
    hits = (order == lax.broadcasted_iota(I32, (N, ROWS), 0)).astype(F32)
    upper = (
        lax.broadcasted_iota(I32, (CH, CH), 0) <= lax.broadcasted_iota(I32, (CH, CH), 1)
    ).astype(BF16)
    before = jnp.zeros((N, 1), F32)
    ranks = []
    for part in range(ROWS // CH):
        hit = hits[:, part * CH : (part + 1) * CH]
        count = jnp.dot(hit.astype(BF16), upper, preferred_element_type=F32) + before
        ranks.append(jnp.sum(count * hit, axis=0, keepdims=True))
        before = before + jnp.sum(hit, axis=1, keepdims=True)
    rank = jnp.concatenate(ranks, axis=1).astype(I32) - 1
    target = order * SLOT + rank

    lane_of = lax.broadcasted_iota(I32, (N, ROWS), 0)
    value = jnp.where(lane_of == rank, (label & 1) + 1, 0).astype(BF16)
    meta = lax.dot_general(
        hits.astype(BF16), value, (((1,), (1,)), ((), ())), preferred_element_type=F32
    )
    meta_send[...] = meta.astype(I32).reshape(N, 1, N)

    def pack(chunk):
        slot = lax.broadcasted_iota(I32, (CH, ROWS), 0) + chunk * CH
        chosen = (slot == target).astype(BF16)
        packed = jnp.dot(chosen, emb[...], preferred_element_type=F32)
        send[chunk * CH : (chunk + 1) * CH, :] = packed.astype(BF16)

    def send_one(k):
        device, chunk, here = partner(k, 1), k // PER, slice(k * SLOT, (k + 1) * SLOT)
        pltpu.make_async_remote_copy(
            src_ref=meta_send.at[k], dst_ref=meta_recv.at[k],
            send_sem=meta_send_sem, recv_sem=meta_sem.at[chunk],
            device_id=device, device_id_type=MESH,
        ).start()
        pltpu.make_async_remote_copy(
            src_ref=send.at[here], dst_ref=recv.at[here],
            send_sem=send_sem, recv_sem=recv_sem.at[chunk],
            device_id=device, device_id_type=MESH,
        ).start()

    fetch.wait()
    pack(0)
    pl.semaphore_wait(barrier, NEAR - 1)
    for k in range(3, NEAR, 3):
        tell(planes_sem, k)
    for chunk in range(NCH):
        if chunk > 0:
            pack(chunk)
        for k in range(max(chunk * PER, 1), (chunk + 1) * PER):
            if k == NEAR:
                pl.semaphore_wait(planes_sem, NEAR // 3)
            send_one(k)

    column = jnp.broadcast_to(target, (N, ROWS)).T
    lanes = lax.broadcasted_iota(I32, (ROWS, N), 1)
    for part in range(SLOTS // N):
        pick[:, part * N : (part + 1) * N] = (column == lanes + part * N).astype(BF16)

    rows[:, E:] = jnp.ones((SLOTS, N), BF16)
    diagonal = lax.broadcasted_iota(I32, (CH, CH), 0) == lax.broadcasted_iota(I32, (CH, CH), 1)
    lane = lax.broadcasted_iota(I32, (CH, N), 1)
    own_slot = lax.broadcasted_iota(I32, (PER, SLOT, N), 1) == lax.broadcasted_iota(
        I32, (PER, SLOT, N), 2
    )
    spread = jnp.ones((N, N), BF16)

    def block(start, size, cols):
        parts = []
        for col in cols:
            score = lax.dot_general(
                left[start : start + size, :], right[col * CH : (col + 1) * CH, :],
                (((1,), (1,)), ((), ())), preferred_element_type=F32,
            )
            weight = jnp.exp(score * 40.0)
            if start == col * CH:
                weight = jnp.where(diagonal, 0.0, weight)
            parts.append(weight.astype(BF16))
        weight = parts[0] if len(parts) == 1 else jnp.concatenate(parts, axis=1)
        return jnp.dot(
            weight, rows[cols[0] * CH : (cols[-1] + 1) * CH, :], preferred_element_type=F32
        )

    def arrive(chunk):
        first = 1 if chunk == 0 else 0
        base, count = chunk * CH + first * SLOT, CH - first * SLOT
        here = slice(chunk * CH, (chunk + 1) * CH)
        pltpu.make_async_copy(
            meta_recv.at[chunk * PER + first : (chunk + 1) * PER],
            meta_recv.at[chunk * PER + first : (chunk + 1) * PER],
            meta_sem.at[chunk],
        ).wait()
        pltpu.make_async_copy(
            recv.at[base : base + count], recv.at[base : base + count], recv_sem.at[chunk]
        ).wait()
        if chunk == 0:
            recv[0:SLOT, :] = send[0:SLOT, :]
            meta_recv[0] = meta_send[0]
        marks = meta_recv[chunk * PER : (chunk + 1) * PER].reshape(PER, 1, N)
        marks = jnp.where(own_slot, jnp.broadcast_to(marks, (PER, SLOT, N)), 0)
        marks = marks.astype(F32).reshape(CH, N).astype(BF16)
        kind = jnp.dot(marks, spread, preferred_element_type=F32).astype(I32)
        kind = jnp.where(kind == 0, 2, kind - 1)
        values = recv[here, :]
        wide = values.astype(F32)
        unit = wide * lax.rsqrt(jnp.sum(wide * wide, axis=1, keepdims=True) + 1e-06)
        unit = unit.astype(BF16)
        rows[here, :E] = values
        left[here, :E] = unit
        right[here, :E] = unit
        left[here, E:] = ((lane < 3) & (lane != kind)).astype(BF16)
        right[here, E:] = jnp.where(lane == kind, -APART, 0.0).astype(BF16)

    for chunk in range(NCH - 1):
        arrive(chunk)
        if chunk < EARLY:
            here = slice(chunk * CH, (chunk + 1) * CH)
            total[here, :] = block(chunk * CH, CH, range(chunk + 1))
        done = min(chunk, EARLY) * CH
        for start in range(0, done, 2 * CH):
            size = min(2 * CH, done - start)
            total[start : start + size, :] += block(start, size, range(chunk, chunk + 1))
    arrive(NCH - 1)

    def return_one(k):
        here = slice(k * SLOT, (k + 1) * SLOT)
        pltpu.make_async_remote_copy(
            src_ref=result.at[here], dst_ref=returned.at[here],
            send_sem=back_sem, recv_sem=return_sem.at[k // PER],
            device_id=partner(k, -1), device_id_type=MESH,
        ).start()

    for chunk in range(NCH):
        here = slice(chunk * CH, (chunk + 1) * CH)
        if chunk < EARLY:
            full = total[here, :] + block(chunk * CH, CH, range(NCH - 1, NCH))
        else:
            full = block(chunk * CH, CH, range(NCH))
        inverse = 1.0 / (1.0 + full[:, E:])
        for part in range(E // N):
            span = slice(part * N, (part + 1) * N)
            mixed = rows[here, span].astype(F32) - full[:, span] * inverse
            result[here, span] = mixed.astype(BF16)
        for k in range(max(chunk * PER, 1), (chunk + 1) * PER):
            return_one(k)
    returned[0:SLOT, :] = result[0:SLOT, :]

    for chunk in range(NCH):
        first = 1 if chunk == 0 else 0
        base, count = chunk * CH + first * SLOT, CH - first * SLOT
        here = slice(chunk * CH, (chunk + 1) * CH)
        pltpu.make_async_copy(
            returned.at[base : base + count], returned.at[base : base + count],
            return_sem.at[chunk],
        ).wait()
        part = jnp.dot(pick[:, here], returned[here, :], preferred_element_type=F32).astype(BF16)
        if chunk == 0:
            out[...] = part
        else:
            out[...] += part

    sent = slice(SLOT, SLOTS)
    pltpu.make_async_copy(send.at[sent], send.at[sent], send_sem).wait()
    pltpu.make_async_copy(meta_send.at[1:N], meta_send.at[1:N], meta_send_sem).wait()
    pltpu.make_async_copy(result.at[sent], result.at[sent], back_sem).wait()


def deliver(held, out, sem):
    copy = pltpu.make_async_copy(held, out, sem)
    copy.start()
    copy.wait()


def on_device(embedding, cluster_of):
    held = pl.pallas_call(
        kernel,
        out_shape=pltpu.VMEM((ROWS, E), BF16),
        in_specs=[pl.BlockSpec(memory_space=pltpu.HBM)] * 2,
        out_specs=pl.BlockSpec(memory_space=pltpu.VMEM),
        scratch_shapes=[
            pltpu.VMEM((ROWS, E), BF16),
            pltpu.VMEM((1, ROWS), I32),
            pltpu.VMEM((SLOTS, E), BF16),
            pltpu.VMEM((N, 1, N), I32),
            pltpu.VMEM((SLOTS, E), BF16),
            pltpu.VMEM((N, 1, N), I32),
            pltpu.VMEM((SLOTS, E + N), BF16),
            pltpu.VMEM((SLOTS, E + N), BF16),
            pltpu.VMEM((SLOTS, E + N), BF16),
            pltpu.VMEM((EARLY * CH, E + N), F32),
            pltpu.VMEM((SLOTS, E), BF16),
            pltpu.VMEM((SLOTS, E), BF16),
            pltpu.VMEM((ROWS, SLOTS), BF16),
            pltpu.SemaphoreType.DMA,
            pltpu.SemaphoreType.DMA,
            pltpu.SemaphoreType.REGULAR,
            pltpu.SemaphoreType.DMA,
            pltpu.SemaphoreType.DMA,
            pltpu.SemaphoreType.DMA,
            pltpu.SemaphoreType.DMA((NCH,)),
            pltpu.SemaphoreType.DMA((NCH,)),
            pltpu.SemaphoreType.DMA((NCH,)),
        ],
        compiler_params=pltpu.CompilerParams(
            collective_id=0, has_side_effects=True, vmem_limit_bytes=56 << 20
        ),
    )(embedding, cluster_of.reshape(1, ROWS))
    return pl.pallas_call(
        deliver,
        out_shape=jax.ShapeDtypeStruct((ROWS, E), BF16),
        in_specs=[pl.BlockSpec(memory_space=pltpu.VMEM)],
        out_specs=pl.BlockSpec(memory_space=pl.ANY),
        scratch_shapes=[pltpu.SemaphoreType.DMA],
    )(held)


def solution(mesh):
    return jax.shard_map(
        on_device,
        mesh=mesh,
        in_specs=(P(("tm", "clus"), None), P(("tm", "clus"))),
        out_specs=P(("tm", "clus"), None),
        check_vma=False,
    )
```

```python
import jax
import jax.numpy as jnp
from jax import lax
from jax.experimental import pallas as pl
from jax.experimental.pallas import tpu as pltpu
from jax.sharding import PartitionSpec as P

MESH = pl.DeviceIdType.MESH
BF16, F32, I32 = jnp.bfloat16, jnp.float32, jnp.int32
N = 128
ROWS = 1024
E = 384
SLOT = 16
SLOTS = N * SLOT
CH = 256
NCH = SLOTS // CH
PER = CH // SLOT
NEAR = 23
EARLY = range(1, 5)
BACK = tuple((i * CH, (i + 1) * CH) for i in range(2, NCH)) + ((CH, 2 * CH), (0, CH))
APART = 16.0


def key_of(dy, dz, dx, dc):
    place, mate = dy * 4 + dz, dx * 2 + dc
    hops = sum(jnp.minimum(d, 4 - d) if isinstance(d, jax.Array) else min(d, 4 - d) for d in (dy, dz, dx))
    mixed = ((place * 8 + mate) * 83) % N
    near = (place * mate == 0) * 1
    return (1 - near) * (1 + (hops < 3)) * N + mixed


SHIFTS = sorted(
    ((dy, dz, dx, dc) for dy in range(4) for dz in range(4) for dx in range(4) for dc in range(2)),
    key=lambda shift: key_of(*shift),
)


def near_line(k):
    return SHIFTS[k][0] == SHIFTS[k][1] == 0


def kernel(
    emb_hbm, labels_hbm, out,
    emb, labels, send, meta_send, recv, meta_recv, rows, left, right, total, result, returned, pick,
    fetch_sem, labels_sem, planes_sem,
    send_sem, meta_send_sem, back_sem, recv_sem, meta_sem, return_sem,
):
    fetch_labels = pltpu.make_async_copy(labels_hbm, labels, labels_sem)
    fetch_labels.start()
    fetch = pltpu.make_async_copy(emb_hbm, emb, fetch_sem)
    fetch.start()

    tm, cl = lax.axis_index("tm"), lax.axis_index("clus")
    y, z, x, c = tm, cl // 8, (cl // 2) % 4, cl % 2
    ys, zs = [lax.rem(y + d, 4) for d in range(4)], [lax.rem(z + d, 4) * 8 for d in range(4)]
    xs, cs = [lax.rem(x + d, 4) * 2 for d in range(4)], [c, 1 - c]
    barrier = pltpu.get_barrier_semaphore()

    def partner(k, sign):
        dy, dz, dx, dc = SHIFTS[k]
        return (ys[sign * dy % 4], zs[sign * dz % 4] + (xs[sign * dx % 4] + cs[dc]))

    def tell(sem, k):
        pl.semaphore_signal(sem, inc=1, device_id=partner(k, 1), device_id_type=MESH)

    for k in range(1, NEAR):
        tell(barrier, k)

    fetch_labels.wait()
    label = labels[...]
    owner = label >> 1
    dy, dz = ((owner >> 5) - y) & 3, ((owner >> 3) - z) & 3
    dx, dc = ((owner >> 1) - x) & 3, (owner - c) & 1
    shift = lax.broadcasted_iota(I32, (N, 1), 0)
    keys = key_of(shift >> 5, (shift >> 3) & 3, (shift >> 1) & 3, shift & 1)
    ahead = (keys < key_of(dy, dz, dx, dc)).astype(F32)
    order = jnp.sum(ahead, axis=0, keepdims=True).astype(I32)
    hits = (order == lax.broadcasted_iota(I32, (N, ROWS), 0)).astype(F32)
    upper = (
        lax.broadcasted_iota(I32, (CH, CH), 0) <= lax.broadcasted_iota(I32, (CH, CH), 1)
    ).astype(BF16)
    before = jnp.zeros((N, 1), F32)
    ranks = []
    for part in range(ROWS // CH):
        hit = hits[:, part * CH : (part + 1) * CH]
        count = jnp.dot(hit.astype(BF16), upper, preferred_element_type=F32) + before
        ranks.append(jnp.sum(count * hit, axis=0, keepdims=True))
        before = before + jnp.sum(hit, axis=1, keepdims=True)
    rank = jnp.concatenate(ranks, axis=1).astype(I32) - 1
    target = order * SLOT + rank

    lane_of = lax.broadcasted_iota(I32, (N, ROWS), 0)
    value = jnp.where(lane_of == rank, (label & 1) + 1, 0).astype(BF16)
    meta = lax.dot_general(
        hits.astype(BF16), value, (((1,), (1,)), ((), ())), preferred_element_type=F32
    )
    meta_send[...] = meta.astype(I32).reshape(N, 1, N)

    def pack(chunk):
        slot = lax.broadcasted_iota(I32, (CH, ROWS), 0) + chunk * CH
        chosen = (slot == target).astype(BF16)
        packed = jnp.dot(chosen, emb[...], preferred_element_type=F32)
        send[chunk * CH : (chunk + 1) * CH, :] = packed.astype(BF16)

    def send_one(k):
        device, chunk, here = partner(k, 1), k // PER, slice(k * SLOT, (k + 1) * SLOT)
        pltpu.make_async_remote_copy(
            src_ref=meta_send.at[k], dst_ref=meta_recv.at[k],
            send_sem=meta_send_sem, recv_sem=meta_sem.at[chunk],
            device_id=device, device_id_type=MESH,
        ).start()
        pltpu.make_async_remote_copy(
            src_ref=send.at[here], dst_ref=recv.at[here],
            send_sem=send_sem, recv_sem=recv_sem.at[chunk],
            device_id=device, device_id_type=MESH,
        ).start()

    fetch.wait()
    pack(0)
    pl.semaphore_wait(barrier, NEAR - 1)
    line = [k for k in range(1, NEAR) if near_line(k)]
    for k in line:
        tell(planes_sem, k)
    for chunk in range(NCH):
        if chunk > 0:
            pack(chunk)
        for k in range(max(chunk * PER, 1), (chunk + 1) * PER):
            if k == NEAR:
                pl.semaphore_wait(planes_sem, len(line))
            send_one(k)

    column = jnp.broadcast_to(target, (N, ROWS)).T
    lanes = lax.broadcasted_iota(I32, (ROWS, N), 1)
    for part in range(SLOTS // N):
        pick[:, part * N : (part + 1) * N] = (column == lanes + part * N).astype(BF16)

    rows[:, E:] = jnp.ones((SLOTS, N), BF16)
    diagonal = lax.broadcasted_iota(I32, (CH, CH), 0) == lax.broadcasted_iota(I32, (CH, CH), 1)
    lane = lax.broadcasted_iota(I32, (CH, N), 1)
    own_slot = lax.broadcasted_iota(I32, (PER, SLOT, N), 1) == lax.broadcasted_iota(
        I32, (PER, SLOT, N), 2
    )
    spread = jnp.ones((N, N), BF16)

    def block(start, size, cols):
        parts = []
        for col in cols:
            score = lax.dot_general(
                left[start : start + size, :], right[col * CH : (col + 1) * CH, :],
                (((1,), (1,)), ((), ())), preferred_element_type=F32,
            )
            weight = jnp.exp(score * 40.0)
            if start == col * CH:
                weight = jnp.where(diagonal, 0.0, weight)
            parts.append(weight.astype(BF16))
        weight = parts[0] if len(parts) == 1 else jnp.concatenate(parts, axis=1)
        return jnp.dot(
            weight, rows[cols[0] * CH : (cols[-1] + 1) * CH, :], preferred_element_type=F32
        )

    def arrive(chunk):
        first = 1 if chunk == 0 else 0
        base, count = chunk * CH + first * SLOT, CH - first * SLOT
        here = slice(chunk * CH, (chunk + 1) * CH)
        pltpu.make_async_copy(
            meta_recv.at[chunk * PER + first : (chunk + 1) * PER],
            meta_recv.at[chunk * PER + first : (chunk + 1) * PER],
            meta_sem.at[chunk],
        ).wait()
        pltpu.make_async_copy(
            recv.at[base : base + count], recv.at[base : base + count], recv_sem.at[chunk]
        ).wait()
        if chunk == 0:
            recv[0:SLOT, :] = send[0:SLOT, :]
            meta_recv[0] = meta_send[0]
        marks = meta_recv[chunk * PER : (chunk + 1) * PER].reshape(PER, 1, N)
        marks = jnp.where(own_slot, jnp.broadcast_to(marks, (PER, SLOT, N)), 0)
        marks = marks.astype(F32).reshape(CH, N).astype(BF16)
        kind = jnp.dot(marks, spread, preferred_element_type=F32).astype(I32)
        kind = jnp.where(kind == 0, 2, kind - 1)
        values = recv[here, :]
        wide = values.astype(F32)
        unit = wide * lax.rsqrt(jnp.sum(wide * wide, axis=1, keepdims=True) + 1e-06)
        unit = unit.astype(BF16)
        rows[here, :E] = values
        left[here, :E] = unit
        right[here, :E] = unit
        left[here, E:] = ((lane < 3) & (lane != kind)).astype(BF16)
        right[here, E:] = jnp.where(lane == kind, -APART, 0.0).astype(BF16)

    for chunk in range(NCH - 1):
        arrive(chunk)
        if chunk in EARLY:
            here = slice((chunk - EARLY[0]) * CH, (chunk - EARLY[0] + 1) * CH)
            total[here, :] = block(chunk * CH, CH, range(chunk + 1))
        done = max(min(chunk, EARLY[-1] + 1) - EARLY[0], 0) * CH
        for start in range(0, done, 2 * CH):
            size = min(2 * CH, done - start)
            total[start : start + size, :] += block(
                start + EARLY[0] * CH, size, range(chunk, chunk + 1)
            )
    arrive(NCH - 1)

    def return_one(k):
        here = slice(k * SLOT, (k + 1) * SLOT)
        pltpu.make_async_remote_copy(
            src_ref=result.at[here], dst_ref=returned.at[here],
            send_sem=back_sem, recv_sem=return_sem.at[[k * SLOT in range(*part) for part in BACK].index(True)],
            device_id=partner(k, -1), device_id_type=MESH,
        ).start()

    def finish(start, size):
        here = slice(start, start + size)
        if start // CH in EARLY:
            there = slice(start - EARLY[0] * CH, start - EARLY[0] * CH + size)
            full = total[there, :] + block(start, size, range(NCH - 1, NCH))
        else:
            full = block(start, size, range(NCH))
        inverse = 1.0 / (1.0 + full[:, E:])
        for part in range(E // N):
            span = slice(part * N, (part + 1) * N)
            mixed = rows[here, span].astype(F32) - full[:, span] * inverse
            result[here, span] = mixed.astype(BF16)
        for k in range(max(start // SLOT, NEAR), (start + size) // SLOT):
            return_one(k)

    finish(CH, N)
    finish(CH + N, N)
    for start in range(2 * CH, SLOTS, CH):
        finish(start, CH)
    finish(0, CH)
    for k in range(1, NEAR):
        return_one(k)
    returned[0:SLOT, :] = result[0:SLOT, :]

    for index, (begin, end) in enumerate(BACK):
        base = max(begin, SLOT)
        pltpu.make_async_copy(
            returned.at[base:end], returned.at[base:end], return_sem.at[index]
        ).wait()
        part = jnp.dot(pick[:, begin:end], returned[begin:end, :], preferred_element_type=F32)
        if index == 0:
            out[...] = part.astype(BF16)
        else:
            out[...] += part.astype(BF16)

    sent = slice(SLOT, SLOTS)
    pltpu.make_async_copy(send.at[sent], send.at[sent], send_sem).wait()
    pltpu.make_async_copy(meta_send.at[1:N], meta_send.at[1:N], meta_send_sem).wait()
    pltpu.make_async_copy(result.at[sent], result.at[sent], back_sem).wait()


def deliver(held, out, sem):
    copy = pltpu.make_async_copy(held, out, sem)
    copy.start()
    copy.wait()


def on_device(embedding, cluster_of):
    held = pl.pallas_call(
        kernel,
        out_shape=pltpu.VMEM((ROWS, E), BF16),
        in_specs=[pl.BlockSpec(memory_space=pltpu.HBM)] * 2,
        out_specs=pl.BlockSpec(memory_space=pltpu.VMEM),
        scratch_shapes=[
            pltpu.VMEM((ROWS, E), BF16),
            pltpu.VMEM((1, ROWS), I32),
            pltpu.VMEM((SLOTS, E), BF16),
            pltpu.VMEM((N, 1, N), I32),
            pltpu.VMEM((SLOTS, E), BF16),
            pltpu.VMEM((N, 1, N), I32),
            pltpu.VMEM((SLOTS, E + N), BF16),
            pltpu.VMEM((SLOTS, E + N), BF16),
            pltpu.VMEM((SLOTS, E + N), BF16),
            pltpu.VMEM((len(EARLY) * CH, E + N), F32),
            pltpu.VMEM((SLOTS, E), BF16),
            pltpu.VMEM((SLOTS, E), BF16),
            pltpu.VMEM((ROWS, SLOTS), BF16),
            pltpu.SemaphoreType.DMA,
            pltpu.SemaphoreType.DMA,
            pltpu.SemaphoreType.REGULAR,
            pltpu.SemaphoreType.DMA,
            pltpu.SemaphoreType.DMA,
            pltpu.SemaphoreType.DMA,
            pltpu.SemaphoreType.DMA((NCH,)),
            pltpu.SemaphoreType.DMA((NCH,)),
            pltpu.SemaphoreType.DMA((len(BACK),)),
        ],
        compiler_params=pltpu.CompilerParams(
            collective_id=0, has_side_effects=True, vmem_limit_bytes=56 << 20
        ),
    )(embedding, cluster_of.reshape(1, ROWS))
    return pl.pallas_call(
        deliver,
        out_shape=jax.ShapeDtypeStruct((ROWS, E), BF16),
        in_specs=[pl.BlockSpec(memory_space=pltpu.VMEM)],
        out_specs=pl.BlockSpec(memory_space=pl.ANY),
        scratch_shapes=[pltpu.SemaphoreType.DMA],
        compiler_params=pltpu.CompilerParams(vmem_limit_bytes=2 << 20),
    )(held)


def solution(mesh):
    return jax.shard_map(
        on_device,
        mesh=mesh,
        in_specs=(P(("tm", "clus"), None), P(("tm", "clus"))),
        out_specs=P(("tm", "clus"), None),
        check_vma=False,
    )
```

```python
import jax
import jax.numpy as jnp
from jax import lax
from jax.experimental import pallas as pl
from jax.experimental.pallas import tpu as pltpu
from jax.sharding import PartitionSpec as P

MESH = pl.DeviceIdType.MESH
BF16, F32, I32 = jnp.bfloat16, jnp.float32, jnp.int32
N = 128
ROWS = 1024
E = 384
SLOT = 16
SLOTS = N * SLOT
CH = 256
NCH = SLOTS // CH
PER = CH // SLOT
NEAR = 23
EARLY = range(1, 3)
BACK = tuple((i * CH, (i + 1) * CH) for i in range(2, NCH)) + ((0, 2 * CH),)
APART = 16.0


def key_of(dy, dz, dx, dc):
    place, mate = dy * 4 + dz, dx * 2 + dc
    hops = sum(jnp.minimum(d, 4 - d) if isinstance(d, jax.Array) else min(d, 4 - d) for d in (dy, dz, dx))
    mixed = ((place * 8 + mate) * 83) % N
    near = (place * mate == 0) * 1
    return (1 - near) * (1 + (hops < 3)) * N + mixed


SHIFTS = sorted(
    ((dy, dz, dx, dc) for dy in range(4) for dz in range(4) for dx in range(4) for dc in range(2)),
    key=lambda shift: key_of(*shift),
)


def near_line(k):
    return SHIFTS[k][0] == SHIFTS[k][1] == 0


def kernel(
    emb_hbm, labels_hbm, out,
    emb, labels, send, meta_send, recv, meta_recv, rows, left, right, total, result, returned, pick,
    fetch_sem, labels_sem, planes_sem,
    send_sem, meta_send_sem, back_sem, recv_sem, meta_sem, return_sem,
):
    fetch_labels = pltpu.make_async_copy(labels_hbm, labels, labels_sem)
    fetch_labels.start()
    fetch = pltpu.make_async_copy(emb_hbm, emb, fetch_sem)
    fetch.start()

    tm, cl = lax.axis_index("tm"), lax.axis_index("clus")
    y, z, x, c = tm, cl // 8, (cl // 2) % 4, cl % 2
    ys, zs = [lax.rem(y + d, 4) for d in range(4)], [lax.rem(z + d, 4) * 8 for d in range(4)]
    xs, cs = [lax.rem(x + d, 4) * 2 for d in range(4)], [c, 1 - c]
    barrier = pltpu.get_barrier_semaphore()

    def partner(k, sign):
        dy, dz, dx, dc = SHIFTS[k]
        return (ys[sign * dy % 4], zs[sign * dz % 4] + (xs[sign * dx % 4] + cs[dc]))

    def tell(sem, k):
        pl.semaphore_signal(sem, inc=1, device_id=partner(k, 1), device_id_type=MESH)

    for k in range(1, NEAR):
        tell(barrier, k)

    fetch_labels.wait()
    label = labels[...]
    owner = label >> 1
    dy, dz = ((owner >> 5) - y) & 3, ((owner >> 3) - z) & 3
    dx, dc = ((owner >> 1) - x) & 3, (owner - c) & 1
    shift = lax.broadcasted_iota(I32, (N, 1), 0)
    keys = key_of(shift >> 5, (shift >> 3) & 3, (shift >> 1) & 3, shift & 1)
    ahead = (keys < key_of(dy, dz, dx, dc)).astype(F32)
    order = jnp.sum(ahead, axis=0, keepdims=True).astype(I32)
    hits = (order == lax.broadcasted_iota(I32, (N, ROWS), 0)).astype(F32)
    upper = (
        lax.broadcasted_iota(I32, (CH, CH), 0) <= lax.broadcasted_iota(I32, (CH, CH), 1)
    ).astype(BF16)
    before = jnp.zeros((N, 1), F32)
    ranks = []
    for part in range(ROWS // CH):
        hit = hits[:, part * CH : (part + 1) * CH]
        count = jnp.dot(hit.astype(BF16), upper, preferred_element_type=F32) + before
        ranks.append(jnp.sum(count * hit, axis=0, keepdims=True))
        before = before + jnp.sum(hit, axis=1, keepdims=True)
    rank = jnp.concatenate(ranks, axis=1).astype(I32) - 1
    target = order * SLOT + rank

    lane_of = lax.broadcasted_iota(I32, (N, ROWS), 0)
    value = jnp.where(lane_of == rank, (label & 1) + 1, 0).astype(BF16)
    meta = lax.dot_general(
        hits.astype(BF16), value, (((1,), (1,)), ((), ())), preferred_element_type=F32
    )
    meta_send[...] = meta.astype(I32).reshape(N, 1, N)

    def pack(chunk):
        slot = lax.broadcasted_iota(I32, (CH, ROWS), 0) + chunk * CH
        chosen = (slot == target).astype(BF16)
        packed = jnp.dot(chosen, emb[...], preferred_element_type=F32)
        send[chunk * CH : (chunk + 1) * CH, :] = packed.astype(BF16)

    def send_one(k):
        device, chunk, here = partner(k, 1), k // PER, slice(k * SLOT, (k + 1) * SLOT)
        pltpu.make_async_remote_copy(
            src_ref=meta_send.at[k], dst_ref=meta_recv.at[k],
            send_sem=meta_send_sem, recv_sem=meta_sem.at[chunk],
            device_id=device, device_id_type=MESH,
        ).start()
        pltpu.make_async_remote_copy(
            src_ref=send.at[here], dst_ref=recv.at[here],
            send_sem=send_sem, recv_sem=recv_sem.at[chunk],
            device_id=device, device_id_type=MESH,
        ).start()

    fetch.wait()
    pack(0)
    pl.semaphore_wait(barrier, NEAR - 1)
    line = [k for k in range(1, NEAR) if near_line(k)]
    for k in line:
        tell(planes_sem, k)
    for chunk in range(NCH):
        if chunk > 0:
            pack(chunk)
        for k in range(max(chunk * PER, 1), (chunk + 1) * PER):
            if k == NEAR:
                pl.semaphore_wait(planes_sem, len(line))
            send_one(k)

    column = jnp.broadcast_to(target, (N, ROWS)).T
    lanes = lax.broadcasted_iota(I32, (ROWS, N), 1)
    for part in range(SLOTS // N):
        pick[:, part * N : (part + 1) * N] = (column == lanes + part * N).astype(BF16)

    rows[:, E:] = jnp.ones((SLOTS, N), BF16)
    diagonal = lax.broadcasted_iota(I32, (CH, CH), 0) == lax.broadcasted_iota(I32, (CH, CH), 1)
    lane = lax.broadcasted_iota(I32, (CH, N), 1)
    own_slot = lax.broadcasted_iota(I32, (PER, SLOT, N), 1) == lax.broadcasted_iota(
        I32, (PER, SLOT, N), 2
    )
    spread = jnp.ones((N, N), BF16)

    def block(start, size, cols):
        parts = []
        for col in cols:
            score = lax.dot_general(
                left[start : start + size, :], right[col * CH : (col + 1) * CH, :],
                (((1,), (1,)), ((), ())), preferred_element_type=F32,
            )
            weight = jnp.exp(score * 40.0)
            if start == col * CH:
                weight = jnp.where(diagonal, 0.0, weight)
            parts.append(weight.astype(BF16))
        weight = parts[0] if len(parts) == 1 else jnp.concatenate(parts, axis=1)
        return jnp.dot(
            weight, rows[cols[0] * CH : (cols[-1] + 1) * CH, :], preferred_element_type=F32
        )

    def arrive(chunk):
        first = 1 if chunk == 0 else 0
        base, count = chunk * CH + first * SLOT, CH - first * SLOT
        here = slice(chunk * CH, (chunk + 1) * CH)
        pltpu.make_async_copy(
            meta_recv.at[chunk * PER + first : (chunk + 1) * PER],
            meta_recv.at[chunk * PER + first : (chunk + 1) * PER],
            meta_sem.at[chunk],
        ).wait()
        pltpu.make_async_copy(
            recv.at[base : base + count], recv.at[base : base + count], recv_sem.at[chunk]
        ).wait()
        if chunk == 0:
            recv[0:SLOT, :] = send[0:SLOT, :]
            meta_recv[0] = meta_send[0]
        marks = meta_recv[chunk * PER : (chunk + 1) * PER].reshape(PER, 1, N)
        marks = jnp.where(own_slot, jnp.broadcast_to(marks, (PER, SLOT, N)), 0)
        marks = marks.astype(F32).reshape(CH, N).astype(BF16)
        kind = jnp.dot(marks, spread, preferred_element_type=F32).astype(I32)
        kind = jnp.where(kind == 0, 2, kind - 1)
        values = recv[here, :]
        wide = values.astype(F32)
        unit = wide * lax.rsqrt(jnp.sum(wide * wide, axis=1, keepdims=True) + 1e-06)
        unit = unit.astype(BF16)
        rows[here, :E] = values
        left[here, :E] = unit
        right[here, :E] = unit
        left[here, E:] = ((lane < 3) & (lane != kind)).astype(BF16)
        right[here, E:] = jnp.where(lane == kind, -APART, 0.0).astype(BF16)

    for chunk in range(NCH - 1):
        arrive(chunk)
        if chunk in EARLY:
            here = slice((chunk - EARLY[0]) * CH, (chunk - EARLY[0] + 1) * CH)
            total[here, :] = block(chunk * CH, CH, range(chunk + 1))
        done = max(min(chunk, EARLY[-1] + 1) - EARLY[0], 0) * CH
        for start in range(0, done, 2 * CH):
            size = min(2 * CH, done - start)
            total[start : start + size, :] += block(
                start + EARLY[0] * CH, size, range(chunk, chunk + 1)
            )
    arrive(NCH - 1)

    def return_one(k):
        here = slice(k * SLOT, (k + 1) * SLOT)
        pltpu.make_async_remote_copy(
            src_ref=result.at[here], dst_ref=returned.at[here],
            send_sem=back_sem, recv_sem=return_sem.at[[k * SLOT in range(*part) for part in BACK].index(True)],
            device_id=partner(k, -1), device_id_type=MESH,
        ).start()

    def finish(start, size):
        here = slice(start, start + size)
        if start // CH in EARLY:
            there = slice(start - EARLY[0] * CH, start - EARLY[0] * CH + size)
            full = total[there, :] + block(start, size, range(NCH - 1, NCH))
        else:
            full = block(start, size, range(NCH))
        inverse = 1.0 / (1.0 + full[:, E:])
        for part in range(E // N):
            span = slice(part * N, (part + 1) * N)
            mixed = rows[here, span].astype(F32) - full[:, span] * inverse
            result[here, span] = mixed.astype(BF16)
        for k in range(max(start // SLOT, NEAR), (start + size) // SLOT):
            return_one(k)

    finish(CH + N, N)
    for start in range(2 * CH, SLOTS, CH):
        finish(start, CH)
    finish(CH, N)
    finish(0, CH)
    for k in range(1, NEAR):
        return_one(k)
    returned[0:SLOT, :] = result[0:SLOT, :]

    for index, (begin, end) in enumerate(BACK):
        base = max(begin, SLOT)
        pltpu.make_async_copy(
            returned.at[base:end], returned.at[base:end], return_sem.at[index]
        ).wait()
        part = jnp.dot(pick[:, begin:end], returned[begin:end, :], preferred_element_type=F32)
        if index == 0:
            out[...] = part.astype(BF16)
        else:
            out[...] += part.astype(BF16)

    sent = slice(SLOT, SLOTS)
    pltpu.make_async_copy(send.at[sent], send.at[sent], send_sem).wait()
    pltpu.make_async_copy(meta_send.at[1:N], meta_send.at[1:N], meta_send_sem).wait()
    pltpu.make_async_copy(result.at[sent], result.at[sent], back_sem).wait()


def deliver(held, out, sem):
    copy = pltpu.make_async_copy(held, out, sem)
    copy.start()
    copy.wait()


def on_device(embedding, cluster_of):
    held = pl.pallas_call(
        kernel,
        out_shape=pltpu.VMEM((ROWS, E), BF16),
        in_specs=[pl.BlockSpec(memory_space=pltpu.HBM)] * 2,
        out_specs=pl.BlockSpec(memory_space=pltpu.VMEM),
        scratch_shapes=[
            pltpu.VMEM((ROWS, E), BF16),
            pltpu.VMEM((1, ROWS), I32),
            pltpu.VMEM((SLOTS, E), BF16),
            pltpu.VMEM((N, 1, N), I32),
            pltpu.VMEM((SLOTS, E), BF16),
            pltpu.VMEM((N, 1, N), I32),
            pltpu.VMEM((SLOTS, E + N), BF16),
            pltpu.VMEM((SLOTS, E + N), BF16),
            pltpu.VMEM((SLOTS, E + N), BF16),
            pltpu.VMEM((len(EARLY) * CH, E + N), F32),
            pltpu.VMEM((SLOTS, E), BF16),
            pltpu.VMEM((SLOTS, E), BF16),
            pltpu.VMEM((ROWS, SLOTS), BF16),
            pltpu.SemaphoreType.DMA,
            pltpu.SemaphoreType.DMA,
            pltpu.SemaphoreType.REGULAR,
            pltpu.SemaphoreType.DMA,
            pltpu.SemaphoreType.DMA,
            pltpu.SemaphoreType.DMA,
            pltpu.SemaphoreType.DMA((NCH,)),
            pltpu.SemaphoreType.DMA((NCH,)),
            pltpu.SemaphoreType.DMA((len(BACK),)),
        ],
        compiler_params=pltpu.CompilerParams(
            collective_id=0, has_side_effects=True, vmem_limit_bytes=56 << 20
        ),
    )(embedding, cluster_of.reshape(1, ROWS))
    return pl.pallas_call(
        deliver,
        out_shape=jax.ShapeDtypeStruct((ROWS, E), BF16),
        in_specs=[pl.BlockSpec(memory_space=pltpu.VMEM)],
        out_specs=pl.BlockSpec(memory_space=pl.ANY),
        scratch_shapes=[pltpu.SemaphoreType.DMA],
        compiler_params=pltpu.CompilerParams(vmem_limit_bytes=2 << 20),
    )(held)


def solution(mesh):
    return jax.shard_map(
        on_device,
        mesh=mesh,
        in_specs=(P(("tm", "clus"), None), P(("tm", "clus"))),
        out_specs=P(("tm", "clus"), None),
        check_vma=False,
    )
```

```python
import jax
import jax.numpy as jnp
from jax import lax
from jax.experimental import pallas as pl
from jax.experimental.pallas import tpu as pltpu
from jax.sharding import PartitionSpec as P

MESH = pl.DeviceIdType.MESH
BF16, F32, I32 = jnp.bfloat16, jnp.float32, jnp.int32
N = 128
ROWS = 1024
E = 384
SLOT = 16
SLOTS = N * SLOT
CH = 256
NCH = SLOTS // CH
PER = CH // SLOT
NEAR = 23
EARLY = range(1, 3)
BACK = tuple((i * CH, (i + 1) * CH) for i in range(2, NCH)) + ((0, 2 * CH),)
APART = 16.0


def key_of(dy, dz, dx, dc):
    place, mate = dy * 4 + dz, dx * 2 + dc
    hops = sum(jnp.minimum(d, 4 - d) if isinstance(d, jax.Array) else min(d, 4 - d) for d in (dy, dz, dx))
    mixed = ((place * 8 + mate) * 117) % N
    near = (place * mate == 0) * 1
    return (1 - near) * (1 + (hops < 3)) * N + mixed


SHIFTS = sorted(
    ((dy, dz, dx, dc) for dy in range(4) for dz in range(4) for dx in range(4) for dc in range(2)),
    key=lambda shift: key_of(*shift),
)


def near_line(k):
    return SHIFTS[k][0] == SHIFTS[k][1] == 0


def kernel(
    emb_hbm, labels_hbm, out,
    emb, labels, send, meta_send, recv, meta_recv, rows, left, right, total, result, returned, pick,
    fetch_sem, labels_sem, planes_sem,
    send_sem, meta_send_sem, back_sem, recv_sem, meta_sem, return_sem,
):
    fetch_labels = pltpu.make_async_copy(labels_hbm, labels, labels_sem)
    fetch_labels.start()
    fetch = pltpu.make_async_copy(emb_hbm, emb, fetch_sem)
    fetch.start()

    tm, cl = lax.axis_index("tm"), lax.axis_index("clus")
    y, z, x, c = tm, cl // 8, (cl // 2) % 4, cl % 2
    ys, zs = [lax.rem(y + d, 4) for d in range(4)], [lax.rem(z + d, 4) * 8 for d in range(4)]
    xs, cs = [lax.rem(x + d, 4) * 2 for d in range(4)], [c, 1 - c]
    barrier = pltpu.get_barrier_semaphore()

    def partner(k, sign):
        dy, dz, dx, dc = SHIFTS[k]
        return (ys[sign * dy % 4], zs[sign * dz % 4] + (xs[sign * dx % 4] + cs[dc]))

    def tell(sem, k):
        pl.semaphore_signal(sem, inc=1, device_id=partner(k, 1), device_id_type=MESH)

    for k in range(1, NEAR):
        tell(barrier, k)

    fetch_labels.wait()
    label = labels[...]
    owner = label >> 1
    dy, dz = ((owner >> 5) - y) & 3, ((owner >> 3) - z) & 3
    dx, dc = ((owner >> 1) - x) & 3, (owner - c) & 1
    shift = lax.broadcasted_iota(I32, (N, 1), 0)
    keys = key_of(shift >> 5, (shift >> 3) & 3, (shift >> 1) & 3, shift & 1)
    ahead = (keys < key_of(dy, dz, dx, dc)).astype(F32)
    order = jnp.sum(ahead, axis=0, keepdims=True).astype(I32)
    hits = (order == lax.broadcasted_iota(I32, (N, ROWS), 0)).astype(F32)
    upper = (
        lax.broadcasted_iota(I32, (CH, CH), 0) <= lax.broadcasted_iota(I32, (CH, CH), 1)
    ).astype(BF16)
    before = jnp.zeros((N, 1), F32)
    ranks = []
    for part in range(ROWS // CH):
        hit = hits[:, part * CH : (part + 1) * CH]
        count = jnp.dot(hit.astype(BF16), upper, preferred_element_type=F32) + before
        ranks.append(jnp.sum(count * hit, axis=0, keepdims=True))
        before = before + jnp.sum(hit, axis=1, keepdims=True)
    rank = jnp.concatenate(ranks, axis=1).astype(I32) - 1
    target = order * SLOT + rank

    lane_of = lax.broadcasted_iota(I32, (N, ROWS), 0)
    value = jnp.where(lane_of == rank, (label & 1) + 1, 0).astype(BF16)
    meta = lax.dot_general(
        hits.astype(BF16), value, (((1,), (1,)), ((), ())), preferred_element_type=F32
    )
    meta_send[...] = meta.astype(I32).reshape(N, 1, N)

    def pack(chunk):
        slot = lax.broadcasted_iota(I32, (CH, ROWS), 0) + chunk * CH
        chosen = (slot == target).astype(BF16)
        packed = jnp.dot(chosen, emb[...], preferred_element_type=F32)
        send[chunk * CH : (chunk + 1) * CH, :] = packed.astype(BF16)

    def send_one(k):
        device, chunk, here = partner(k, 1), k // PER, slice(k * SLOT, (k + 1) * SLOT)
        pltpu.make_async_remote_copy(
            src_ref=meta_send.at[k], dst_ref=meta_recv.at[k],
            send_sem=meta_send_sem, recv_sem=meta_sem.at[chunk],
            device_id=device, device_id_type=MESH,
        ).start()
        pltpu.make_async_remote_copy(
            src_ref=send.at[here], dst_ref=recv.at[here],
            send_sem=send_sem, recv_sem=recv_sem.at[chunk],
            device_id=device, device_id_type=MESH,
        ).start()

    fetch.wait()
    pack(0)
    pl.semaphore_wait(barrier, NEAR - 1)
    line = [k for k in range(1, NEAR) if near_line(k)]
    for k in line:
        tell(planes_sem, k)
    for chunk in range(NCH):
        if chunk > 0:
            pack(chunk)
        for k in range(max(chunk * PER, 1), (chunk + 1) * PER):
            if k == NEAR:
                pl.semaphore_wait(planes_sem, len(line))
            send_one(k)

    column = jnp.broadcast_to(target, (N, ROWS)).T
    lanes = lax.broadcasted_iota(I32, (ROWS, N), 1)
    for part in range(SLOTS // N):
        pick[:, part * N : (part + 1) * N] = (column == lanes + part * N).astype(BF16)

    rows[:, E:] = jnp.ones((SLOTS, N), BF16)
    diagonal = lax.broadcasted_iota(I32, (CH, CH), 0) == lax.broadcasted_iota(I32, (CH, CH), 1)
    lane = lax.broadcasted_iota(I32, (CH, N), 1)
    own_slot = lax.broadcasted_iota(I32, (PER, SLOT, N), 1) == lax.broadcasted_iota(
        I32, (PER, SLOT, N), 2
    )
    spread = jnp.ones((N, N), BF16)

    def block(start, size, cols):
        parts = []
        for col in cols:
            score = lax.dot_general(
                left[start : start + size, :], right[col * CH : (col + 1) * CH, :],
                (((1,), (1,)), ((), ())), preferred_element_type=F32,
            )
            weight = jnp.exp(score * 40.0)
            if start == col * CH:
                weight = jnp.where(diagonal, 0.0, weight)
            parts.append(weight.astype(BF16))
        weight = parts[0] if len(parts) == 1 else jnp.concatenate(parts, axis=1)
        return jnp.dot(
            weight, rows[cols[0] * CH : (cols[-1] + 1) * CH, :], preferred_element_type=F32
        )

    def arrive(chunk):
        first = 1 if chunk == 0 else 0
        base, count = chunk * CH + first * SLOT, CH - first * SLOT
        here = slice(chunk * CH, (chunk + 1) * CH)
        pltpu.make_async_copy(
            meta_recv.at[chunk * PER + first : (chunk + 1) * PER],
            meta_recv.at[chunk * PER + first : (chunk + 1) * PER],
            meta_sem.at[chunk],
        ).wait()
        pltpu.make_async_copy(
            recv.at[base : base + count], recv.at[base : base + count], recv_sem.at[chunk]
        ).wait()
        if chunk == 0:
            recv[0:SLOT, :] = send[0:SLOT, :]
            meta_recv[0] = meta_send[0]
        marks = meta_recv[chunk * PER : (chunk + 1) * PER].reshape(PER, 1, N)
        marks = jnp.where(own_slot, jnp.broadcast_to(marks, (PER, SLOT, N)), 0)
        marks = marks.astype(F32).reshape(CH, N).astype(BF16)
        kind = jnp.dot(marks, spread, preferred_element_type=F32).astype(I32)
        kind = jnp.where(kind == 0, 2, kind - 1)
        values = recv[here, :]
        wide = values.astype(F32)
        unit = wide * lax.rsqrt(jnp.sum(wide * wide, axis=1, keepdims=True) + 1e-06)
        unit = unit.astype(BF16)
        rows[here, :E] = values
        left[here, :E] = unit
        right[here, :E] = unit
        left[here, E:] = ((lane < 3) & (lane != kind)).astype(BF16)
        right[here, E:] = jnp.where(lane == kind, -APART, 0.0).astype(BF16)

    for chunk in range(NCH - 1):
        arrive(chunk)
        if chunk in EARLY:
            here = slice((chunk - EARLY[0]) * CH, (chunk - EARLY[0] + 1) * CH)
            total[here, :] = block(chunk * CH, CH, range(chunk + 1))
        done = max(min(chunk, EARLY[-1] + 1) - EARLY[0], 0) * CH
        for start in range(0, done, 2 * CH):
            size = min(2 * CH, done - start)
            total[start : start + size, :] += block(
                start + EARLY[0] * CH, size, range(chunk, chunk + 1)
            )
    arrive(NCH - 1)

    def return_one(k):
        here = slice(k * SLOT, (k + 1) * SLOT)
        pltpu.make_async_remote_copy(
            src_ref=result.at[here], dst_ref=returned.at[here],
            send_sem=back_sem, recv_sem=return_sem.at[[k * SLOT in range(*part) for part in BACK].index(True)],
            device_id=partner(k, -1), device_id_type=MESH,
        ).start()

    def finish(start, size):
        here = slice(start, start + size)
        if start // CH in EARLY:
            there = slice(start - EARLY[0] * CH, start - EARLY[0] * CH + size)
            full = total[there, :] + block(start, size, range(NCH - 1, NCH))
        else:
            full = block(start, size, range(NCH))
        inverse = 1.0 / (1.0 + full[:, E:])
        for part in range(E // N):
            span = slice(part * N, (part + 1) * N)
            mixed = rows[here, span].astype(F32) - full[:, span] * inverse
            result[here, span] = mixed.astype(BF16)
        for k in range(max(start // SLOT, NEAR), (start + size) // SLOT):
            return_one(k)

    finish(CH + N, N)
    for start in range(2 * CH, SLOTS, CH):
        finish(start, CH)
    finish(CH, N)
    finish(0, CH)
    for k in range(1, NEAR):
        return_one(k)
    returned[0:SLOT, :] = result[0:SLOT, :]

    for index, (begin, end) in enumerate(BACK):
        base = max(begin, SLOT)
        pltpu.make_async_copy(
            returned.at[base:end], returned.at[base:end], return_sem.at[index]
        ).wait()
        part = jnp.dot(pick[:, begin:end], returned[begin:end, :], preferred_element_type=F32)
        if index == 0:
            out[...] = part.astype(BF16)
        else:
            out[...] += part.astype(BF16)

    sent = slice(SLOT, SLOTS)
    pltpu.make_async_copy(send.at[sent], send.at[sent], send_sem).wait()
    pltpu.make_async_copy(meta_send.at[1:N], meta_send.at[1:N], meta_send_sem).wait()
    pltpu.make_async_copy(result.at[sent], result.at[sent], back_sem).wait()


def deliver(held, out, sem):
    copy = pltpu.make_async_copy(held, out, sem)
    copy.start()
    copy.wait()


def on_device(embedding, cluster_of):
    held = pl.pallas_call(
        kernel,
        out_shape=pltpu.VMEM((ROWS, E), BF16),
        in_specs=[pl.BlockSpec(memory_space=pltpu.HBM)] * 2,
        out_specs=pl.BlockSpec(memory_space=pltpu.VMEM),
        scratch_shapes=[
            pltpu.VMEM((ROWS, E), BF16),
            pltpu.VMEM((1, ROWS), I32),
            pltpu.VMEM((SLOTS, E), BF16),
            pltpu.VMEM((N, 1, N), I32),
            pltpu.VMEM((SLOTS, E), BF16),
            pltpu.VMEM((N, 1, N), I32),
            pltpu.VMEM((SLOTS, E + N), BF16),
            pltpu.VMEM((SLOTS, E + N), BF16),
            pltpu.VMEM((SLOTS, E + N), BF16),
            pltpu.VMEM((len(EARLY) * CH, E + N), F32),
            pltpu.VMEM((SLOTS, E), BF16),
            pltpu.VMEM((SLOTS, E), BF16),
            pltpu.VMEM((ROWS, SLOTS), BF16),
            pltpu.SemaphoreType.DMA,
            pltpu.SemaphoreType.DMA,
            pltpu.SemaphoreType.REGULAR,
            pltpu.SemaphoreType.DMA,
            pltpu.SemaphoreType.DMA,
            pltpu.SemaphoreType.DMA,
            pltpu.SemaphoreType.DMA((NCH,)),
            pltpu.SemaphoreType.DMA((NCH,)),
            pltpu.SemaphoreType.DMA((len(BACK),)),
        ],
        compiler_params=pltpu.CompilerParams(
            collective_id=0, has_side_effects=True, vmem_limit_bytes=56 << 20
        ),
    )(embedding, cluster_of.reshape(1, ROWS))
    return pl.pallas_call(
        deliver,
        out_shape=jax.ShapeDtypeStruct((ROWS, E), BF16),
        in_specs=[pl.BlockSpec(memory_space=pltpu.VMEM)],
        out_specs=pl.BlockSpec(memory_space=pl.ANY),
        scratch_shapes=[pltpu.SemaphoreType.DMA],
        compiler_params=pltpu.CompilerParams(vmem_limit_bytes=2 << 20),
    )(held)


def solution(mesh):
    return jax.shard_map(
        on_device,
        mesh=mesh,
        in_specs=(P(("tm", "clus"), None), P(("tm", "clus"))),
        out_specs=P(("tm", "clus"), None),
        check_vma=False,
    )
```

```python
import jax
import jax.numpy as jnp
from jax import lax
from jax.experimental import pallas as pl
from jax.experimental.pallas import tpu as pltpu
from jax.sharding import PartitionSpec as P

MESH = pl.DeviceIdType.MESH
BF16, F32, I32 = jnp.bfloat16, jnp.float32, jnp.int32
N = 128
ROWS = 1024
E = 384
SLOT = 16
SLOTS = N * SLOT
CH = 256
NCH = SLOTS // CH
PER = CH // SLOT
NEAR = 23
EARLY = range(1, 3)
BACK = tuple((i * CH, (i + 1) * CH) for i in range(2, NCH)) + ((0, 2 * CH),)
APART = 16.0


def key_of(dy, dz, dx, dc):
    place, mate = dy * 4 + dz, dx * 2 + dc
    hops = sum(jnp.minimum(d, 4 - d) if isinstance(d, jax.Array) else min(d, 4 - d) for d in (dy, dz, dx))
    mixed = ((place * 8 + mate) * 37) % N
    near = (place * mate == 0) * 1
    return (1 - near) * (1 + (hops < 3)) * N + mixed


SHIFTS = sorted(
    ((dy, dz, dx, dc) for dy in range(4) for dz in range(4) for dx in range(4) for dc in range(2)),
    key=lambda shift: key_of(*shift),
)


def near_line(k):
    return SHIFTS[k][0] == SHIFTS[k][1] == 0


def kernel(
    emb_hbm, labels_hbm, out,
    emb, labels, send, meta_send, recv, meta_recv, rows, left, right, total, result, returned, pick,
    fetch_sem, labels_sem, planes_sem,
    send_sem, meta_send_sem, back_sem, recv_sem, meta_sem, return_sem,
):
    fetch_labels = pltpu.make_async_copy(labels_hbm, labels, labels_sem)
    fetch_labels.start()
    fetch = pltpu.make_async_copy(emb_hbm, emb, fetch_sem)
    fetch.start()

    tm, cl = lax.axis_index("tm"), lax.axis_index("clus")
    y, z, x, c = tm, cl // 8, (cl // 2) % 4, cl % 2
    ys, zs = [lax.rem(y + d, 4) for d in range(4)], [lax.rem(z + d, 4) * 8 for d in range(4)]
    xs, cs = [lax.rem(x + d, 4) * 2 for d in range(4)], [c, 1 - c]
    barrier = pltpu.get_barrier_semaphore()

    def partner(k, sign):
        dy, dz, dx, dc = SHIFTS[k]
        return (ys[sign * dy % 4], zs[sign * dz % 4] + (xs[sign * dx % 4] + cs[dc]))

    def tell(sem, k):
        pl.semaphore_signal(sem, inc=1, device_id=partner(k, 1), device_id_type=MESH)

    for k in range(1, NEAR):
        tell(barrier, k)

    fetch_labels.wait()
    label = labels[...]
    owner = label >> 1
    dy, dz = ((owner >> 5) - y) & 3, ((owner >> 3) - z) & 3
    dx, dc = ((owner >> 1) - x) & 3, (owner - c) & 1
    shift = lax.broadcasted_iota(I32, (N, 1), 0)
    keys = key_of(shift >> 5, (shift >> 3) & 3, (shift >> 1) & 3, shift & 1)
    ahead = (keys < key_of(dy, dz, dx, dc)).astype(F32)
    order = jnp.sum(ahead, axis=0, keepdims=True).astype(I32)
    hits = (order == lax.broadcasted_iota(I32, (N, ROWS), 0)).astype(F32)
    upper = (
        lax.broadcasted_iota(I32, (CH, CH), 0) <= lax.broadcasted_iota(I32, (CH, CH), 1)
    ).astype(BF16)
    before = jnp.zeros((N, 1), F32)
    ranks = []
    for part in range(ROWS // CH):
        hit = hits[:, part * CH : (part + 1) * CH]
        count = jnp.dot(hit.astype(BF16), upper, preferred_element_type=F32) + before
        ranks.append(jnp.sum(count * hit, axis=0, keepdims=True))
        before = before + jnp.sum(hit, axis=1, keepdims=True)
    rank = jnp.concatenate(ranks, axis=1).astype(I32) - 1
    target = order * SLOT + rank

    lane_of = lax.broadcasted_iota(I32, (N, ROWS), 0)
    value = jnp.where(lane_of == rank, (label & 1) + 1, 0).astype(BF16)
    meta = lax.dot_general(
        hits.astype(BF16), value, (((1,), (1,)), ((), ())), preferred_element_type=F32
    )
    meta_send[...] = meta.astype(I32).reshape(N, 1, N)

    def pack(chunk):
        slot = lax.broadcasted_iota(I32, (CH, ROWS), 0) + chunk * CH
        chosen = (slot == target).astype(BF16)
        packed = jnp.dot(chosen, emb[...], preferred_element_type=F32)
        send[chunk * CH : (chunk + 1) * CH, :] = packed.astype(BF16)

    def send_one(k):
        device, chunk, here = partner(k, 1), k // PER, slice(k * SLOT, (k + 1) * SLOT)
        pltpu.make_async_remote_copy(
            src_ref=meta_send.at[k], dst_ref=meta_recv.at[k],
            send_sem=meta_send_sem, recv_sem=meta_sem.at[chunk],
            device_id=device, device_id_type=MESH,
        ).start()
        pltpu.make_async_remote_copy(
            src_ref=send.at[here], dst_ref=recv.at[here],
            send_sem=send_sem, recv_sem=recv_sem.at[chunk],
            device_id=device, device_id_type=MESH,
        ).start()

    fetch.wait()
    pack(0)
    pl.semaphore_wait(barrier, NEAR - 1)
    line = [k for k in range(1, NEAR) if near_line(k)]
    for k in line:
        tell(planes_sem, k)
    for chunk in range(NCH):
        if chunk > 0:
            pack(chunk)
        for k in range(max(chunk * PER, 1), (chunk + 1) * PER):
            if k == NEAR:
                pl.semaphore_wait(planes_sem, len(line))
            send_one(k)

    column = jnp.broadcast_to(target, (N, ROWS)).T
    lanes = lax.broadcasted_iota(I32, (ROWS, N), 1)
    for part in range(SLOTS // N):
        pick[:, part * N : (part + 1) * N] = (column == lanes + part * N).astype(BF16)

    rows[:, E:] = jnp.ones((SLOTS, N), BF16)
    diagonal = lax.broadcasted_iota(I32, (CH, CH), 0) == lax.broadcasted_iota(I32, (CH, CH), 1)
    lane = lax.broadcasted_iota(I32, (CH, N), 1)
    own_slot = lax.broadcasted_iota(I32, (PER, SLOT, N), 1) == lax.broadcasted_iota(
        I32, (PER, SLOT, N), 2
    )
    spread = jnp.ones((N, N), BF16)

    def block(start, size, cols):
        parts = []
        for col in cols:
            score = lax.dot_general(
                left[start : start + size, :], right[col * CH : (col + 1) * CH, :],
                (((1,), (1,)), ((), ())), preferred_element_type=F32,
            )
            weight = jnp.exp(score * 40.0)
            if start == col * CH:
                weight = jnp.where(diagonal, 0.0, weight)
            parts.append(weight.astype(BF16))
        weight = parts[0] if len(parts) == 1 else jnp.concatenate(parts, axis=1)
        return jnp.dot(
            weight, rows[cols[0] * CH : (cols[-1] + 1) * CH, :], preferred_element_type=F32
        )

    def arrive(chunk):
        first = 1 if chunk == 0 else 0
        base, count = chunk * CH + first * SLOT, CH - first * SLOT
        here = slice(chunk * CH, (chunk + 1) * CH)
        pltpu.make_async_copy(
            meta_recv.at[chunk * PER + first : (chunk + 1) * PER],
            meta_recv.at[chunk * PER + first : (chunk + 1) * PER],
            meta_sem.at[chunk],
        ).wait()
        pltpu.make_async_copy(
            recv.at[base : base + count], recv.at[base : base + count], recv_sem.at[chunk]
        ).wait()
        if chunk == 0:
            recv[0:SLOT, :] = send[0:SLOT, :]
            meta_recv[0] = meta_send[0]
        marks = meta_recv[chunk * PER : (chunk + 1) * PER].reshape(PER, 1, N)
        marks = jnp.where(own_slot, jnp.broadcast_to(marks, (PER, SLOT, N)), 0)
        marks = marks.astype(F32).reshape(CH, N).astype(BF16)
        kind = jnp.dot(marks, spread, preferred_element_type=F32).astype(I32)
        kind = jnp.where(kind == 0, 2, kind - 1)
        values = recv[here, :]
        wide = values.astype(F32)
        unit = wide * lax.rsqrt(jnp.sum(wide * wide, axis=1, keepdims=True) + 1e-06)
        unit = unit.astype(BF16)
        rows[here, :E] = values
        left[here, :E] = unit
        right[here, :E] = unit
        left[here, E:] = ((lane < 3) & (lane != kind)).astype(BF16)
        right[here, E:] = jnp.where(lane == kind, -APART, 0.0).astype(BF16)

    for chunk in range(NCH - 1):
        arrive(chunk)
        if chunk in EARLY:
            here = slice((chunk - EARLY[0]) * CH, (chunk - EARLY[0] + 1) * CH)
            total[here, :] = block(chunk * CH, CH, range(chunk + 1))
        done = max(min(chunk, EARLY[-1] + 1) - EARLY[0], 0) * CH
        for start in range(0, done, 2 * CH):
            size = min(2 * CH, done - start)
            total[start : start + size, :] += block(
                start + EARLY[0] * CH, size, range(chunk, chunk + 1)
            )
    arrive(NCH - 1)

    def return_one(k):
        here = slice(k * SLOT, (k + 1) * SLOT)
        pltpu.make_async_remote_copy(
            src_ref=result.at[here], dst_ref=returned.at[here],
            send_sem=back_sem, recv_sem=return_sem.at[[k * SLOT in range(*part) for part in BACK].index(True)],
            device_id=partner(k, -1), device_id_type=MESH,
        ).start()

    def finish(start, size):
        here = slice(start, start + size)
        if start // CH in EARLY:
            there = slice(start - EARLY[0] * CH, start - EARLY[0] * CH + size)
            full = total[there, :] + block(start, size, range(NCH - 1, NCH))
        else:
            full = block(start, size, range(NCH))
        inverse = 1.0 / (1.0 + full[:, E:])
        for part in range(E // N):
            span = slice(part * N, (part + 1) * N)
            mixed = rows[here, span].astype(F32) - full[:, span] * inverse
            result[here, span] = mixed.astype(BF16)
        for k in range(max(start // SLOT, NEAR), (start + size) // SLOT):
            return_one(k)

    finish(CH + N, N)
    for start in range(2 * CH, SLOTS, CH):
        finish(start, CH)
    finish(CH, N)
    finish(0, CH)
    for k in range(1, NEAR):
        return_one(k)
    returned[0:SLOT, :] = result[0:SLOT, :]

    for index, (begin, end) in enumerate(BACK):
        base = max(begin, SLOT)
        pltpu.make_async_copy(
            returned.at[base:end], returned.at[base:end], return_sem.at[index]
        ).wait()
        part = jnp.dot(pick[:, begin:end], returned[begin:end, :], preferred_element_type=F32)
        if index == 0:
            out[...] = part.astype(BF16)
        else:
            out[...] += part.astype(BF16)

    sent = slice(SLOT, SLOTS)
    pltpu.make_async_copy(send.at[sent], send.at[sent], send_sem).wait()
    pltpu.make_async_copy(meta_send.at[1:N], meta_send.at[1:N], meta_send_sem).wait()
    pltpu.make_async_copy(result.at[sent], result.at[sent], back_sem).wait()


def deliver(held, out, sem):
    copy = pltpu.make_async_copy(held, out, sem)
    copy.start()
    copy.wait()


def on_device(embedding, cluster_of):
    held = pl.pallas_call(
        kernel,
        out_shape=pltpu.VMEM((ROWS, E), BF16),
        in_specs=[pl.BlockSpec(memory_space=pltpu.HBM)] * 2,
        out_specs=pl.BlockSpec(memory_space=pltpu.VMEM),
        scratch_shapes=[
            pltpu.VMEM((ROWS, E), BF16),
            pltpu.VMEM((1, ROWS), I32),
            pltpu.VMEM((SLOTS, E), BF16),
            pltpu.VMEM((N, 1, N), I32),
            pltpu.VMEM((SLOTS, E), BF16),
            pltpu.VMEM((N, 1, N), I32),
            pltpu.VMEM((SLOTS, E + N), BF16),
            pltpu.VMEM((SLOTS, E + N), BF16),
            pltpu.VMEM((SLOTS, E + N), BF16),
            pltpu.VMEM((len(EARLY) * CH, E + N), F32),
            pltpu.VMEM((SLOTS, E), BF16),
            pltpu.VMEM((SLOTS, E), BF16),
            pltpu.VMEM((ROWS, SLOTS), BF16),
            pltpu.SemaphoreType.DMA,
            pltpu.SemaphoreType.DMA,
            pltpu.SemaphoreType.REGULAR,
            pltpu.SemaphoreType.DMA,
            pltpu.SemaphoreType.DMA,
            pltpu.SemaphoreType.DMA,
            pltpu.SemaphoreType.DMA((NCH,)),
            pltpu.SemaphoreType.DMA((NCH,)),
            pltpu.SemaphoreType.DMA((len(BACK),)),
        ],
        compiler_params=pltpu.CompilerParams(
            collective_id=0, has_side_effects=True, vmem_limit_bytes=56 << 20
        ),
    )(embedding, cluster_of.reshape(1, ROWS))
    return pl.pallas_call(
        deliver,
        out_shape=jax.ShapeDtypeStruct((ROWS, E), BF16),
        in_specs=[pl.BlockSpec(memory_space=pltpu.VMEM)],
        out_specs=pl.BlockSpec(memory_space=pl.ANY),
        scratch_shapes=[pltpu.SemaphoreType.DMA],
        compiler_params=pltpu.CompilerParams(vmem_limit_bytes=2 << 20),
    )(held)


def solution(mesh):
    return jax.shard_map(
        on_device,
        mesh=mesh,
        in_specs=(P(("tm", "clus"), None), P(("tm", "clus"))),
        out_specs=P(("tm", "clus"), None),
        check_vma=False,
    )
```
